256 devices in a mesh: tok: 64 (over z, y, core), head: 4 (over x).
Axes of the slice: x: 4, y: 4, z: 8, core: 2. Of those that a mesh axis runs over, the one named last changes fastest.
Arguments:
- tokens: bfloat16 [524288, 256], P('tok'), may hold values from -6 to 6
- coords: float32 [3, 524288], P(None, 'tok'), may hold values from -1 to 1, as said below
- latents: bfloat16 [256, 512], replicated, may hold values from -6 to 6
- anchors: float32 [3, 256], replicated, may hold values from -8 to 8
- gamma: float32 [8], P('head'), may hold values from 0.02 to 3
- w_query: bfloat16 [512, 512], P(None, 'head'), may hold values from -0.25 to 0.25
- w_key: bfloat16 [256, 512], P(None, 'head'), may hold values from -0.375 to 0.375
- w_value: bfloat16 [256, 512], P(None, 'head'), may hold values from -0.375 to 0.375
- w_out: bfloat16 [512, 512], P('head'), may hold values from -0.5 to 0.5
- d_update: bfloat16 [256, 512], replicated, may hold values from -6 to 6
Outputs:
- update: bfloat16 [256, 512], replicated
- d_latents: float32 [256, 512], replicated
- d_wq: float32 [512, 512], P(None, 'head')
- d_wk: float32 [256, 512], P(None, 'head')
- d_wv: float32 [256, 512], P(None, 'head')
- d_wo: float32 [512, 512], P('head')
The draws below stay inside these ranges and needn't reach their ends.
Inputs may be any that keep to these rules, and one draw needn't show every extreme that they name: `coords`: x and y are spread over the box; the third coordinate rises with the token index.
All inputs are finite; a program needn't handle non-finite values.
Results may differ from the reference program's by a relative error of at most 0.013.
Values may be sent and summed in bfloat16 or wider, within the bound.
No kernel may reach another device: no remote copies, remote signals or barrier semaphores. Data moves between devices by JAX's collectives and lax.ppermute only.
A program may use at most 128 MiB of HBM per device.

```python
import math
import jax
import jax.numpy as jnp
from jax import lax

LAT = 256
HEADS = 8
HEAD_FEATURES = 64
DL = 512
DT = 256
TOKENS = 524288


def draw_coords(key, part):
    key = jax.random.fold_in(key, 11)
    key_plane, key_depth = jax.random.split(key)
    plane = jax.random.uniform(key_plane, (2, TOKENS), jnp.float32, -1.0, 1.0)
    jitter = jax.random.uniform(key_depth, (TOKENS,), jnp.float32)
    depth = -1.0 + 2.0 * (jnp.arange(TOKENS, dtype=jnp.float32) + jitter) / TOKENS
    return jnp.concatenate([plane, depth[None, :]], axis=0)


def draw_anchors(key, part):
    key = jax.random.fold_in(key, 12)
    base = jax.random.uniform(key, (3, LAT), jnp.float32, -1.0, 1.0)
    return base


def shard_levels(key, dims, pieces, smallest, top_value):
    level, own = 1.0, jax.random.fold_in(key, 6)
    for axis_at, parts in pieces:
        steps = jnp.exp(jax.random.uniform(jax.random.fold_in(own, axis_at), (parts,), jnp.float32, smallest / len(pieces), top_value / len(pieces)))
        level = level * jnp.repeat(steps, dims[axis_at] // parts).reshape([-1 if axis == axis_at else 1 for axis in range(len(dims))])
    return level


def centred(rng, extent, deviation, limit, pieces=(), kind=jnp.bfloat16):
    loudness = shard_levels(rng, extent, pieces, -0.22, 0.18) if pieces else 1.0
    entries = jax.random.normal(rng, extent, jnp.float32) * deviation * loudness
    return jnp.minimum(jnp.maximum(entries, -limit), limit).astype(kind)


def setup_inputs(seed: int = 0) -> dict:
    key_of = jax.random.split(jax.random.key(seed), 11)
    return {
        "tokens": centred(key_of[0], (TOKENS, DT), 1.0, 6.0, ((0, 64),)),
        "coords": draw_coords(jax.random.fold_in(key_of[10], 71), 0),
        "latents": centred(key_of[2], (LAT, DL), 1.0, 6.0),
        "anchors": draw_anchors(jax.random.fold_in(key_of[10], 71), 0),
        "gamma": jnp.clip(jnp.exp(math.log(3.0) - 5.0106353 * jax.random.uniform(key_of[4], (HEADS,), jnp.float32) ** shard_levels(key_of[4], (HEADS,), ((0, 4),), -0.2, 0.2)), 0.02, 3.0),
        "w_query": centred(key_of[5], (DL, DL), DL ** -0.5, 0.25, ((1, 4),)),
        "w_key": centred(key_of[6], (DT, DL), DT ** -0.5, 0.375, ((1, 4),)),
        "w_value": centred(key_of[7], (DT, DL), DT ** -0.5, 0.375, ((1, 4),)),
        "w_out": centred(key_of[8], (DL, DL), (DL // 4) ** -0.5, 0.5, ((0, 4),)),
        "d_update": centred(key_of[9], (LAT, DL), 1.0, 6.0),
    }


def layer_norm(input_rows):
    row_average = lax.optimization_barrier(jnp.mean(input_rows, axis=-1, keepdims=True))
    var = lax.optimization_barrier(jnp.mean((input_rows - row_average) ** 2, axis=-1, keepdims=True))
    return (input_rows - row_average) * lax.rsqrt(var + 1e-05)

def norm_back(input_rows, upstream_gradient):
    row_average = lax.optimization_barrier(jnp.mean(input_rows, axis=-1, keepdims=True))
    var = lax.optimization_barrier(jnp.mean((input_rows - row_average) ** 2, axis=-1, keepdims=True))
    inverse_stddev = lax.rsqrt(var + 1e-05)
    normalized_input = (input_rows - row_average) * inverse_stddev
    return inverse_stddev * (upstream_gradient - lax.optimization_barrier(jnp.mean(upstream_gradient, axis=-1, keepdims=True)) - normalized_input * lax.optimization_barrier(jnp.mean(upstream_gradient * normalized_input, axis=-1, keepdims=True)))

def reference(tokens, coords, latents, anchors, gamma, w_query, w_key, w_value, w_out, d_update):
    f32 = jnp.float32
    bf16 = jnp.bfloat16
    scale = HEAD_FEATURES ** (-0.5)
    lat_norm = layer_norm(latents.astype(f32)).astype(bf16)
    query = (jnp.dot(lat_norm, w_query, preferred_element_type=f32) * scale).astype(bf16)
    q_heads = query.reshape(LAT, HEADS, HEAD_FEATURES).astype(f32)
    anchor_sq = lax.optimization_barrier(jnp.sum(anchors * anchors, axis=0))
    block = min(4096, TOKENS)
    steps_all = jnp.arange(TOKENS // block, dtype=jnp.int32)

    def tile(index):
        start = (index * block).astype(jnp.int32)
        tok_norm = layer_norm(lax.dynamic_slice_in_dim(tokens, start, block, 0).astype(f32)).astype(bf16)
        points = lax.dynamic_slice_in_dim(coords, start, block, 1)
        keys = jnp.dot(tok_norm, w_key, preferred_element_type=f32).astype(bf16)
        values = jnp.dot(tok_norm, w_value, preferred_element_type=f32).astype(bf16)
        k_heads = keys.reshape(block, HEADS, HEAD_FEATURES).astype(f32)
        v_heads = values.reshape(block, HEADS, HEAD_FEATURES).astype(f32)
        cross = jnp.dot(anchors.T, points, precision=lax.Precision.HIGHEST)
        dist = anchor_sq[:, None] + lax.optimization_barrier(jnp.sum(points * points, axis=0))[None, :] - 2.0 * cross
        scores = jnp.einsum('lhd,bhd->hlb', q_heads, k_heads) - gamma[:, None, None] * dist[None]
        return (tok_norm, k_heads, v_heads, scores)

    def forward_step(carry, index):
        run_max, total, accum = carry
        tok_norm, k_heads, v_heads, scores = tile(index)
        new_max = jnp.maximum(run_max, lax.optimization_barrier(jnp.max(scores, axis=2)))
        factor = jnp.exp(run_max - new_max)
        expo = jnp.exp(scores - new_max[:, :, None]).astype(bf16).astype(f32)
        total = total * factor + lax.optimization_barrier(jnp.sum(expo, axis=2))
        accum = accum * factor.T[:, :, None] + jnp.einsum('hlb,bhd->lhd', expo, v_heads)
        return ((new_max, total, accum), None)
    init = (jnp.full((HEADS, LAT), -jnp.inf, f32), jnp.zeros((HEADS, LAT), f32), jnp.zeros((LAT, HEADS, HEAD_FEATURES), f32))
    (row_max, total, accum), _ = lax.scan(forward_step, init, steps_all)
    attn = (accum / total.T[:, :, None]).reshape(LAT, DL).astype(bf16)
    update = jnp.dot(attn, w_out, preferred_element_type=f32).astype(bf16)
    d_attn = jnp.dot(d_update, w_out.T, preferred_element_type=f32).astype(bf16)
    d_wo = jnp.dot(attn.T, d_update, preferred_element_type=f32)
    do_heads = d_attn.reshape(LAT, HEADS, HEAD_FEATURES).astype(f32)
    delta = lax.optimization_barrier(jnp.sum(do_heads * attn.reshape(LAT, HEADS, HEAD_FEATURES).astype(f32), axis=2)).T
    lse = row_max + jnp.log(total)

    def backward_step(carry, index):
        query_gradient, d_key_w, d_value_w = carry
        tok_norm, k_heads, v_heads, scores = tile(index)
        probs = jnp.exp(scores - lse[:, :, None])
        d_probs = jnp.einsum('lhd,bhd->hlb', do_heads, v_heads)
        d_scores = (probs * (d_probs - delta[:, :, None])).astype(bf16).astype(f32)
        probs_b = probs.astype(bf16).astype(f32)
        query_gradient = query_gradient + jnp.einsum('hlb,bhd->lhd', d_scores, k_heads)
        d_keys = jnp.einsum('hlb,lhd->bhd', d_scores, q_heads).reshape(block, DL).astype(bf16)
        d_values = jnp.einsum('hlb,lhd->bhd', probs_b, do_heads).reshape(block, DL).astype(bf16)
        d_key_w = d_key_w + jnp.dot(tok_norm.T, d_keys, preferred_element_type=f32)
        d_value_w = d_value_w + jnp.dot(tok_norm.T, d_values, preferred_element_type=f32)
        return ((query_gradient, d_key_w, d_value_w), None)
    init_back = (jnp.zeros((LAT, HEADS, HEAD_FEATURES), f32), jnp.zeros((DT, DL), f32), jnp.zeros((DT, DL), f32))
    (query_gradient, d_wk, d_wv), _ = lax.scan(backward_step, init_back, steps_all)
    dq_b = (query_gradient.reshape(LAT, DL) * scale).astype(bf16)
    d_wq = jnp.dot(lat_norm.T, dq_b, preferred_element_type=f32)
    d_norm = jnp.dot(dq_b, w_query.T, preferred_element_type=f32)
    d_latents = norm_back(latents.astype(f32), d_norm)
    return (update, d_latents, d_wq, d_wk, d_wv, d_wo)
```

```python
import functools

import jax
import jax.numpy as jnp
from jax import lax
from jax.experimental import pallas as pl
from jax.experimental.pallas import tpu as pltpu
from jax.sharding import Mesh, PartitionSpec as P

f32 = jnp.float32
bf16 = jnp.bfloat16
HS = 64
STAT = 128
Z_MIN = 1e-25
VMEM = 56 * 1024 * 1024
NT = (((1,), (1,)), ((), ()))
TN = (((0,), (0,)), ((), ()))


def nn(a, b):
    return jnp.dot(a, b, preferred_element_type=f32)


def nt(a, b):
    return lax.dot_general(a, b, NT, preferred_element_type=f32)


def tn(a, b):
    return lax.dot_general(a, b, TN, preferred_element_type=f32)


def iota(shape, dim):
    return lax.broadcasted_iota(jnp.int32, shape, dim)


def one_hot(hit):
    return jnp.where(hit, 1.0, 0.0).astype(bf16)


def norm_rows(v):
    mean=jnp.mean(v,axis=-1,keepdims=True)
    d=v-mean
    var=jnp.mean(d*d,axis=-1,keepdims=True)
    return d*lax.rsqrt(var+1e-5)

def column(row, n):
    r=lax.broadcasted_iota(jnp.int32,(n,n),0); c=lax.broadcasted_iota(jnp.int32,(n,n),1)
    return jnp.sum(jnp.where(r==c,jnp.broadcast_to(row,(n,n)),0.0),axis=1,keepdims=True)

def main_kernel(lat, heads, tb, rc, tc, where_ref, gamma_ref, tok_ref, pts_ref, lat_ref, anc_ref, wq_ref, wk_ref, wv_ref, wo_ref, du_ref,
                send_ref, keep_ref, latn_out, q_out, do_out, r_out,
                p_s, r_s, shift_s, anch_s, x_s, eh_s, acc_s, z_s):
    step=pl.program_id(0); steps=pl.num_programs(0)
    width=heads*HS
    rows=heads*lat
    feat=tok_ref.shape[1]
    lane=lax.broadcasted_iota(jnp.int32,(lat,width),1)

    @pl.when(step==0)
    def _():
        latn=norm_rows(lat_ref[...].astype(f32)).astype(bf16)
        latn_out[...]=latn
        q=(nn(latn,wq_ref[...])*(HS**-0.5)).astype(bf16)
        do=nt(du_ref[...],wo_ref[...]).astype(bf16)
        q_out[...]=q; do_out[...]=do
        for k in range(3):
            col=column(anc_ref[k:k+1,:],lat)
            anch_s[k]=jnp.broadcast_to(col,(lat,128))
        box=jnp.zeros((lat,1),f32)
        for k in range(3):
            a=anch_s[k][:,0:1]
            lo=jnp.min(pts_ref[k:k+1,:],axis=1,keepdims=True); hi=jnp.max(pts_ref[k:k+1,:],axis=1,keepdims=True)
            gap=jnp.maximum(jnp.maximum(lo-a,a-hi),0.0)
            box=box+gap*gap
        for h in range(heads):
            mask=(lane>=h*HS)&(lane<(h+1)*HS)
            zero=jnp.zeros((),bf16)
            p=nt(jnp.where(mask,q,zero),wk_ref[...]).astype(bf16)
            r=nt(jnp.where(mask,do,zero),wv_ref[...]).astype(bf16)
            p_s[h*lat:(h+1)*lat,:]=p
            r_s[h*lat:(h+1)*lat,:]=r
            r_out[h*lat:(h+1)*lat,:]=r
            pf=p.astype(f32)
            bound=jnp.sqrt(jnp.sum(pf*pf,axis=1,keepdims=True))*(feat**0.5)-gamma_ref[h]*box
            hi=bound.astype(bf16).astype(f32)
            lo=(bound-hi).astype(bf16).astype(f32)
            shift_s[h*lat:(h+1)*lat,:]=jnp.broadcast_to(hi+lo,(lat,128))
        acc_s[...]=jnp.zeros_like(acc_s)
        z_s[...]=jnp.zeros_like(z_s)

    def rep(a,n): return jnp.concatenate([a]*(n//128),axis=1) if n>128 else a

    def scores(x,pts,h,r0):
        s=nt(p_s[h*lat+r0:h*lat+r0+rc,:],x)
        return s

    def distance(pts,r0,n):
        d=None
        for k in range(3):
            t=rep(anch_s[k,r0:r0+rc,:],n)-pts[k:k+1,:]
            d=t*t if d is None else d+t*t
        return d

    def add_block(start,x,pts):
        for t0 in range(0,tb,tc):
            xt=x[t0:t0+tc,:]
            pt=pts[:,t0:t0+tc]
            for r0 in range(0,lat,rc):
                d=distance(pt,r0,tc)
                for h in range(heads):
                    a=h*lat+r0
                    s=scores(xt,pt,h,r0)
                    g=nt(r_s[a:a+rc,:],xt)
                    e=jnp.exp(s-(gamma_ref[h]*d+rep(shift_s[a:a+rc,:],tc))).astype(bf16)
                    ef=e.astype(f32)
                    part=ef[:,0:128]
                    for j in range(128,tc,128): part=part+ef[:,j:j+128]
                    z_s[a:a+rc,:]+=part
                    eh_s[a:a+rc,t0:t0+tc]=e
                    eh_s[rows+a:rows+a+rc,t0:t0+tc]=(ef*g).astype(bf16)
        acc_s[...]+=nn(eh_s[...],x)

    start=pl.multiple_of(step*tb,tb)
    x=norm_rows(tok_ref[...].astype(f32)).astype(bf16)
    x_s[pl.ds(start,tb),:]=x
    add_block(start,x,pts_ref[:,pl.ds(start,tb)])

    @pl.when(step==steps-1)
    def _():
        low=jnp.min(jnp.sum(z_s[...],axis=1,keepdims=True))

        @pl.when(jnp.logical_not(low>=Z_MIN))
        def _():
            shift_s[...]=jnp.full_like(shift_s,-jnp.inf)
            def top(i,carry):
                at=pl.multiple_of(i*tb,tb)
                xb=x_s[pl.ds(at,tb),:]; pb=pts_ref[:,pl.ds(at,tb)]
                for t0 in range(0,tb,tc):
                    for r0 in range(0,lat,rc):
                        d=distance(pb[:,t0:t0+tc],r0,tc)
                        for h in range(heads):
                            a=h*lat+r0
                            s=scores(xb[t0:t0+tc,:],None,h,r0)-gamma_ref[h]*d
                            shift_s[a:a+rc,:]=jnp.maximum(shift_s[a:a+rc,:],jnp.broadcast_to(jnp.max(s,axis=1,keepdims=True),(rc,128)))
                return carry
            lax.fori_loop(0,steps,top,0)
            m=shift_s[...]
            hi=m.astype(bf16).astype(f32)
            shift_s[...]=hi+(m-hi).astype(bf16).astype(f32)
            acc_s[...]=jnp.zeros_like(acc_s)
            z_s[...]=jnp.zeros_like(z_s)
            def again(i,carry):
                at=pl.multiple_of(i*tb,tb)
                add_block(at,x_s[pl.ds(at,tb),:],pts_ref[:,pl.ds(at,tb)])
                return carry
            lax.fori_loop(0,steps,again,0)

        z=jnp.sum(z_s[...],axis=1,keepdims=True)
        shift=shift_s[...]
        stat=write_stat(z,shift[:,0:1])
        full=jnp.concatenate([acc_s[0:rows,:].astype(bf16),acc_s[rows:2*rows,:].astype(bf16),stat],axis=1)
        core=where_ref[0]
        half=rows//2; each=lat//2
        for out,c in ((send_ref,1-core),(keep_ref,core)):
            ro=lax.broadcasted_iota(jnp.int32,(half,rows),0); co=lax.broadcasted_iota(jnp.int32,(half,rows),1)
            src=((ro>>2)&1)*lat+c*each+((ro>>3)<<2)+(ro&3)
            pick=jnp.where(co==src,1.0,0.0).astype(bf16)
            out[...]=nn(pick,full).astype(bf16)

def main_call(where,gamma,tokens,coords,latents,anchors,wq,wk,wv,wo,du,tb=2048,rc=256,tc=512):
    toks,feat=tokens.shape; lat,dl=latents.shape; heads=gamma.shape[0]; width=heads*HS; rows=heads*lat
    steps=toks//tb
    cols=2*feat+128
    full=lambda a: pl.BlockSpec(a.shape,lambda i:(0,)*a.ndim)
    smem=pl.BlockSpec(memory_space=pltpu.SMEM)
    outs=[jax.ShapeDtypeStruct((rows//2,cols),bf16)]*2+[jax.ShapeDtypeStruct((lat,dl),bf16),jax.ShapeDtypeStruct((lat,width),bf16),jax.ShapeDtypeStruct((lat,width),bf16),jax.ShapeDtypeStruct((rows,feat),bf16)]
    return pl.pallas_call(
        functools.partial(main_kernel,lat,heads,tb,rc,tc),
        grid=(steps,),
        out_shape=outs,
        in_specs=[smem,smem,pl.BlockSpec((tb,feat),lambda i:(i,0))]+[full(a) for a in (coords,latents,anchors,wq,wk,wv,wo,du)],
        out_specs=[full(o) for o in outs],
        scratch_shapes=[pltpu.VMEM((rows,feat),bf16),pltpu.VMEM((rows,feat),bf16),pltpu.VMEM((rows,128),f32),pltpu.VMEM((3,lat,128),f32),
            pltpu.VMEM((toks,feat),bf16),pltpu.VMEM((2*rows,tb),bf16),pltpu.VMEM((2*rows,feat),f32),pltpu.VMEM((rows,128),f32)],
        compiler_params=pltpu.CompilerParams(vmem_limit_bytes=VMEM),
        name="token_pass",
    )(where,gamma,tokens,coords,latents,anchors,wq,wk,wv,wo,du)


def read_stat(stat):
    return stat[:, 0:1] + stat[:, 1:2], stat[:, 2:3] + stat[:, 3:4]


def write_stat(z, shift):
    rows = z.shape[0]
    at = iota((rows, STAT), 1)
    z_hi = z.astype(bf16).astype(f32)
    s_hi = shift.astype(bf16).astype(f32)
    stat = jnp.where(at == 2, s_hi, jnp.where(at == 3, shift - s_hi, 0.0))
    stat = jnp.where(at == 0, z_hi, jnp.where(at == 1, z - z_hi, stat))
    return stat.astype(bf16)


def pair_kernel(a_ref, b_ref, out_ref):
    wide = a_ref.shape[1] - STAT
    za, sa = read_stat(a_ref[:, wide:].astype(f32))
    zb, sb = read_stat(b_ref[:, wide:].astype(f32))
    shift = jnp.maximum(sa, sb)
    wa = jnp.exp(sa - shift)
    wb = jnp.exp(sb - shift)
    out_ref[:, 0:wide] = (a_ref[:, 0:wide].astype(f32) * wa + b_ref[:, 0:wide].astype(f32) * wb).astype(bf16)
    out_ref[:, wide:] = write_stat(za * wa + zb * wb, shift)


def owner_kernel(lat, heads, chips, where_ref, all_ref, r_ref, wk_ref, wv_ref, wo_ref, wq_ref, fg_out, part_out):
    rows = all_ref.shape[0] // chips
    per = rows // heads
    feat = wk_ref.shape[0]
    width = wk_ref.shape[1]
    wide = 2 * feat
    group = where_ref[0] * chips + where_ref[1]
    z, shift = read_stat(all_ref[:, wide:].astype(f32))
    z = z.reshape(chips, rows, 1)
    shift = shift.reshape(chips, rows, 1)
    top = jnp.max(shift, axis=0, keepdims=True)
    w = jnp.exp(shift - top)
    total = jnp.sum(z * w, axis=0)
    sums = jnp.sum(all_ref[:, 0:wide].astype(f32).reshape(chips, rows, wide) * w, axis=0)
    inv = 1.0 / total
    f = sums[:, 0:feat] * inv
    at = iota((rows, heads * lat), 0)
    src = (at // per) * lat + group * per + at % per
    r = nn(one_hot(iota((rows, heads * lat), 1) == src), r_ref[...])
    delta = jnp.sum(f * r, axis=1, keepdims=True)
    g = sums[:, feat:wide] * inv - delta * f
    fb = f.astype(bf16)
    gb = g.astype(bf16)
    fg_out[...] = jnp.concatenate([fb, gb], axis=1)
    mine = iota((rows, width), 1) // HS == iota((rows, width), 0) // per
    o = jnp.where(mine, nn(fb, wv_ref[...]), 0.0).astype(bf16)
    dq = jnp.where(mine, nn(gb, wk_ref[...]) * (HS ** -0.5), 0.0).astype(bf16)
    up = nn(o, wo_ref[...])
    dn = nt(dq, wq_ref[...])
    up = up + pltpu.roll(up, per, 0)
    dn = dn + pltpu.roll(dn, per, 0)
    part_out[...] = jnp.where(iota(up.shape, 0) < per, up, dn).astype(bf16)


def spread_kernel(chips, heads, groups, where_ref, *refs):
    parts, (fg_ref, lat_ref, out_ref) = refs[:groups], refs[groups:]
    rows = fg_ref.shape[0]
    per = rows // heads
    lat = lat_ref.shape[0]
    group = where_ref[0] * chips + where_ref[1]
    tot = parts[0][...].astype(f32)
    for p in parts[1:]:
        tot = tot + p[...].astype(f32)
    at = iota((rows, lat), 0)
    x = nn(one_hot(iota((rows, lat), 1) == group * per + at % per), lat_ref[...])
    mean = jnp.mean(x, axis=-1, keepdims=True)
    d = x - mean
    inv = lax.rsqrt(jnp.mean(d * d, axis=-1, keepdims=True) + 1e-5)
    xhat = d * inv
    back = inv * (tot - jnp.mean(tot, axis=-1, keepdims=True) - xhat * jnp.mean(tot * xhat, axis=-1, keepdims=True))
    ud = jnp.where(iota(tot.shape, 0) < per, tot, back)
    row = jnp.concatenate([fg_ref[...].astype(f32), ud], axis=1)
    block = jnp.concatenate([row, row], axis=0).astype(bf16)
    for s in range(chips // 2):
        out_ref[s * 2 * rows:(s + 1) * 2 * rows, :] = block


def finish_kernel(chips, heads, where_ref, own_ref, other_ref, q_ref, do_ref, latn_ref, wk_ref, wv_ref, du_ref,
                  up_out, dl_out, dwq_out, dwk_out, dwv_out, dwo_out):
    lat, width = q_ref.shape
    feat = wk_ref.shape[0]
    half = own_ref.shape[0]
    rows = half // chips
    per = rows // heads
    core = where_ref[0]

    def place(at):
        c = jnp.where(at < half, core, 1 - core)
        chip = (at % half) // rows
        return (c * chips + chip) * per + at % per, (at % rows) // per

    both = jnp.concatenate([own_ref[...], other_ref[...]], axis=0)
    f = both[:, 0:feat]
    g = both[:, feat:2 * feat]
    ud = both[:, 2 * feat:]
    l, _ = place(iota((2 * half, lat), 0))
    spread = one_hot(l == iota((2 * half, lat), 1))
    _, h = place(iota((2 * half, width), 0))
    mine = h == iota((2 * half, width), 1) // HS
    zero = jnp.zeros((), f32)
    do = jnp.where(mine, nn(spread, do_ref[...]), zero).astype(bf16)
    q = jnp.where(mine, nn(spread, q_ref[...]), zero).astype(bf16)
    dwv_out[...] = tn(f, do)
    dwk_out[...] = tn(g, q)
    o = jnp.where(mine, nn(f, wv_ref[...]), zero).astype(bf16)
    dq = jnp.where(mine, nn(g, wk_ref[...]) * (HS ** -0.5), zero).astype(bf16)
    l, h = place(iota((lat, 2 * half), 1))
    hit = l == iota((lat, 2 * half), 0)
    gather = one_hot(hit)
    o = nn(gather, o).astype(bf16)
    dq = nn(gather, dq).astype(bf16)
    dwo_out[...] = tn(o, du_ref[...])
    dwq_out[...] = tn(latn_ref[...], dq)
    up_out[...] = nn(one_hot(hit & (h == 0)), ud).astype(bf16)
    dl_out[...] = nn(one_hot(hit & (h == 1)), ud)


def small(kernel, outs, smem, name):
    one = pl.BlockSpec(memory_space=pltpu.VMEM)
    params = pltpu.CompilerParams(vmem_limit_bytes=VMEM)
    shapes = [jax.ShapeDtypeStruct(s, t) for s, t in outs]

    def call(*args):
        specs = [pl.BlockSpec(memory_space=pltpu.SMEM)] * smem + [one] * (len(args) - smem)
        return pl.pallas_call(
            kernel, out_shape=shapes, in_specs=specs, out_specs=[one] * len(shapes), compiler_params=params, name=name
        )(*args)

    return call


def shards(tokens, coords, latents, anchors, gamma, w_query, w_key, w_value, w_out, d_update):
    lat, dl = latents.shape
    feat = tokens.shape[1]
    heads = gamma.shape[0]
    width = heads * HS
    chips = lax.axis_size("chip")
    groups = lax.axis_size("head")
    half = heads * lat // 2
    rows = half // chips
    wide = 2 * feat
    where = jnp.stack([lax.axis_index("core"), lax.axis_index("chip")]).astype(jnp.int32)
    swap = [(0, 1), (1, 0)]

    send, keep, latn, q, do, r = main_call(
        where, gamma, tokens, coords, latents, anchors, w_query, w_key, w_value, w_out, d_update
    )
    got = lax.ppermute(send, "core", swap)
    (pair,) = small(pair_kernel, [((half, wide + STAT), bf16)], 0, "pair_sum")(keep, got)
    shares = lax.all_to_all(pair.reshape(chips, rows, wide + STAT), "chip", 0, 0, tiled=True)
    fg, part = small(
        functools.partial(owner_kernel, lat, heads, chips), [((rows, wide), bf16), ((rows, dl), bf16)], 1, "owner_rows"
    )(where, shares.reshape(half, wide + STAT), r, w_key, w_value, w_out, w_query)
    parts = [part]
    for k in range(1, groups):
        parts.append(lax.ppermute(part, "head", [(i, (i + k) % groups) for i in range(groups)]))
    (copies,) = small(
        functools.partial(spread_kernel, chips, heads, groups), [((half, wide + dl), bf16)], 1, "spread_rows"
    )(where, *parts, fg, latents)
    own = lax.all_to_all(copies.reshape(chips, rows, wide + dl), "chip", 0, 0, tiled=True).reshape(half, wide + dl)
    other = lax.ppermute(own, "core", swap)
    outs = [((lat, dl), bf16), ((lat, dl), f32), ((dl, width), f32), ((feat, width), f32), ((feat, width), f32), ((width, dl), f32)]
    return tuple(
        small(functools.partial(finish_kernel, chips, heads), outs, 1, "finish")(
            where, own, other, q, do, latn, w_key, w_value, d_update
        )
    )


def solution(mesh):
    toks, head = mesh.devices.shape
    fine = Mesh(mesh.devices.reshape(toks // 2, 2, head), ("chip", "core", "head"))
    tok = ("chip", "core")
    return jax.shard_map(
        shards,
        mesh=fine,
        in_specs=(
            P(tok, None),
            P(None, tok),
            P(),
            P(),
            P("head"),
            P(None, "head"),
            P(None, "head"),
            P(None, "head"),
            P("head", None),
            P(),
        ),
        out_specs=(P(), P(), P(None, "head"), P(None, "head"), P(None, "head"), P("head", None)),
        check_vma=False,
    )
```

```python
import functools

import jax
import jax.numpy as jnp
from jax import lax
from jax.experimental import pallas as pl
from jax.experimental.pallas import tpu as pltpu
from jax.sharding import Mesh, PartitionSpec as P

f32 = jnp.float32
bf16 = jnp.bfloat16
HS = 64
STAT = 128
Z_MIN = 1e-25
MAIN_VMEM = 58 * 1024 * 1024
VMEM = 10 * 1024 * 1024
NT = (((1,), (1,)), ((), ()))
TN = (((0,), (0,)), ((), ()))


def nn(a, b):
    return jnp.dot(a, b, preferred_element_type=f32)


def nt(a, b):
    return lax.dot_general(a, b, NT, preferred_element_type=f32)


def tn(a, b):
    return lax.dot_general(a, b, TN, preferred_element_type=f32)


def iota(shape, dim):
    return lax.broadcasted_iota(jnp.int32, shape, dim)


def one_hot(hit):
    return jnp.where(hit, 1.0, 0.0).astype(bf16)


def norm_rows(v):
    mean = jnp.mean(v, axis=-1, keepdims=True)
    d = v - mean
    var = jnp.mean(d * d, axis=-1, keepdims=True)
    return d * lax.rsqrt(var + 1e-5)


def column(row, n):
    return jnp.sum(
        jnp.where(iota((n, n), 0) == iota((n, n), 1), jnp.broadcast_to(row, (n, n)), 0.0), axis=1, keepdims=True
    )


def two_parts(v):
    high = v.astype(bf16).astype(f32)
    return high + (v - high).astype(bf16).astype(f32)


def token_kernel(lat, heads, tb, tc, core_ref, gamma_ref, tok_ref, pts_ref, lat_ref, anc_ref, wq_ref, wk_ref, wv_ref,
                 wo_ref, du_ref, send_ref, keep_ref, latn_out, q_out, do_out, r_out,
                 anc_s, p_s, r_s, shift_s, x_s, acc_s, z_s):
    step = pl.program_id(0)
    steps = pl.num_programs(0)
    rows = heads * lat
    feat = tok_ref.shape[1]

    @pl.when(step == 0)
    def _():
        latn = norm_rows(lat_ref[...].astype(f32)).astype(bf16)
        latn_out[...] = latn
        q = (nn(latn, wq_ref[...]) * (HS ** -0.5)).astype(bf16)
        do = nt(du_ref[...], wo_ref[...]).astype(bf16)
        q_out[...] = q
        do_out[...] = do
        box = jnp.zeros((lat, 1), f32)
        for k in range(3):
            a = column(anc_ref[k:k + 1, :], lat)
            anc_s[k] = jnp.broadcast_to(a, (lat, 128))
            low = jnp.min(pts_ref[k:k + 1, :], axis=1, keepdims=True)
            high = jnp.max(pts_ref[k:k + 1, :], axis=1, keepdims=True)
            gap = jnp.maximum(jnp.maximum(low - a, a - high), 0.0)
            box = box + gap * gap
        for h in range(heads):
            at = slice(h * lat, (h + 1) * lat)
            mine = iota(q.shape, 1) // HS == h
            p = nt(jnp.where(mine, q, jnp.zeros((), bf16)), wk_ref[...]).astype(bf16)
            r = nt(jnp.where(mine, do, jnp.zeros((), bf16)), wv_ref[...]).astype(bf16)
            p_s[at, :] = p
            r_s[at, :] = r
            r_out[at, :] = r
            size = p.astype(f32)
            size = jnp.sqrt(jnp.sum(size * size, axis=1, keepdims=True)) * (feat ** 0.5)
            shift_s[at, :] = jnp.broadcast_to(two_parts(size - gamma_ref[h] * box), (lat, 128))
        acc_s[...] = jnp.zeros_like(acc_s)
        z_s[...] = jnp.zeros_like(z_s)

    def wide(a):
        return jnp.concatenate([a] * (tc // 128), axis=1)

    def scores(x, pts):
        s = nt(p_s[...], x)
        dist = None
        for k in range(3):
            t = wide(anc_s[k]) - pts[k:k + 1, :]
            dist = t * t if dist is None else dist + t * t
        heads_s = []
        for h in range(heads):
            at = slice(h * lat, (h + 1) * lat)
            heads_s.append(s[at] - (gamma_ref[h] * dist + wide(shift_s[at, :])))
        return jnp.concatenate(heads_s, axis=0)

    def add_chunk(x, pts):
        s = scores(x, pts)
        g = nt(r_s[...], x)
        e = jnp.exp(s).astype(bf16)
        ef = e.astype(f32)
        part = ef[:, 0:128]
        for j in range(128, tc, 128):
            part = part + ef[:, j:j + 128]
        z_s[...] += part
        acc_s[...] += nn(jnp.concatenate([e, (ef * g).astype(bf16)], axis=0), x)

    start = pl.multiple_of(step * tb, tb)
    for t in range(0, tb, tc):
        x = norm_rows(tok_ref[t:t + tc, :].astype(f32)).astype(bf16)
        x_s[pl.ds(start + t, tc), :] = x
        add_chunk(x, pts_ref[:, pl.ds(start + t, tc)])

    @pl.when(step == steps - 1)
    def _():
        low = jnp.min(jnp.sum(z_s[...], axis=1, keepdims=True))

        @pl.when(jnp.logical_not(low >= Z_MIN))
        def _():
            chunks = x_s.shape[0] // tc
            shift_s[...] = jnp.zeros_like(shift_s)
            z_s[...] = jnp.full_like(z_s, -jnp.inf)

            def top(i, carry):
                at = pl.multiple_of(i * tc, tc)
                s = scores(x_s[pl.ds(at, tc), :], pts_ref[:, pl.ds(at, tc)])
                for j in range(0, tc, 128):
                    z_s[...] = jnp.maximum(z_s[...], s[:, j:j + 128])
                return carry

            lax.fori_loop(0, chunks, top, 0)
            shift_s[...] = jnp.broadcast_to(two_parts(jnp.max(z_s[...], axis=1, keepdims=True)), shift_s.shape)
            acc_s[...] = jnp.zeros_like(acc_s)
            z_s[...] = jnp.zeros_like(z_s)

            def again(i, carry):
                at = pl.multiple_of(i * tc, tc)
                add_chunk(x_s[pl.ds(at, tc), :], pts_ref[:, pl.ds(at, tc)])
                return carry

            lax.fori_loop(0, chunks, again, 0)

        stat = write_stat(jnp.sum(z_s[...], axis=1, keepdims=True), shift_s[:, 0:1])
        full = jnp.concatenate([acc_s[0:rows, :].astype(bf16), acc_s[rows:2 * rows, :].astype(bf16), stat], axis=1)
        core = core_ref[0]
        half = rows // 2
        per = 4
        at = iota((half, rows), 0)
        for out, c in ((send_ref, 1 - core), (keep_ref, core)):
            src = (at // per % heads) * lat + c * (lat // 2) + at // (per * heads) * per + at % per
            out[...] = nn(one_hot(iota((half, rows), 1) == src), full).astype(bf16)


def token_pass(core, gamma, tokens, coords, latents, anchors, wq, wk, wv, wo, du):
    toks, feat = tokens.shape
    lat, dl = latents.shape
    heads = gamma.shape[0]
    width = heads * HS
    rows = heads * lat
    tb = min(4096, toks)
    tc = min(256, tb)
    cols = 2 * feat + STAT

    def full(a):
        return pl.BlockSpec(a.shape, lambda i: (0,) * len(a.shape))

    smem = pl.BlockSpec(memory_space=pltpu.SMEM)
    shapes = [(rows // 2, cols)] * 2 + [(lat, dl), (lat, width), (lat, width), (rows, feat)]
    outs = [jax.ShapeDtypeStruct(s, bf16) for s in shapes]
    held = (coords, latents, anchors, wq, wk, wv, wo, du)
    return pl.pallas_call(
        functools.partial(token_kernel, lat, heads, tb, tc),
        grid=(toks // tb,),
        out_shape=outs,
        in_specs=[smem, smem, pl.BlockSpec((tb, feat), lambda i: (i, 0))] + [full(a) for a in held],
        out_specs=[full(o) for o in outs],
        scratch_shapes=[
            pltpu.VMEM((3, lat, 128), f32),
            pltpu.VMEM((rows, feat), bf16),
            pltpu.VMEM((rows, feat), bf16),
            pltpu.VMEM((rows, 128), f32),
            pltpu.VMEM((toks, feat), bf16),
            pltpu.VMEM((2 * rows, feat), f32),
            pltpu.VMEM((rows, 128), f32),
        ],
        compiler_params=pltpu.CompilerParams(vmem_limit_bytes=MAIN_VMEM),
        name="token_pass",
    )(core, gamma, tokens, *held)


def read_stat(stat):
    return stat[:, 0:1] + stat[:, 1:2], stat[:, 2:3] + stat[:, 3:4]


def write_stat(z, shift):
    rows = z.shape[0]
    at = iota((rows, STAT), 1)
    z_hi = z.astype(bf16).astype(f32)
    s_hi = shift.astype(bf16).astype(f32)
    stat = jnp.where(at == 2, s_hi, jnp.where(at == 3, shift - s_hi, 0.0))
    stat = jnp.where(at == 0, z_hi, jnp.where(at == 1, z - z_hi, stat))
    return stat.astype(bf16)


def pair_kernel(a_ref, b_ref, out_ref):
    wide = a_ref.shape[1] - STAT
    za, sa = read_stat(a_ref[:, wide:].astype(f32))
    zb, sb = read_stat(b_ref[:, wide:].astype(f32))
    shift = jnp.maximum(sa, sb)
    wa = jnp.exp(sa - shift)
    wb = jnp.exp(sb - shift)
    out_ref[:, 0:wide] = (a_ref[:, 0:wide].astype(f32) * wa + b_ref[:, 0:wide].astype(f32) * wb).astype(bf16)
    out_ref[:, wide:] = write_stat(za * wa + zb * wb, shift)


def owner_kernel(lat, heads, chips, core_ref, chip_ref, all_ref, r_ref, wk_ref, wv_ref, wo_ref, wq_ref, fg_out, part_out):
    rows = all_ref.shape[0] // chips
    per = rows // heads
    feat = wk_ref.shape[0]
    width = wk_ref.shape[1]
    wide = 2 * feat
    group = core_ref[0] * chips + chip_ref[0]
    z, shift = read_stat(all_ref[:, wide:].astype(f32))
    z = z.reshape(chips, rows, 1)
    shift = shift.reshape(chips, rows, 1)
    top = jnp.max(shift, axis=0, keepdims=True)
    w = jnp.exp(shift - top)
    total = jnp.sum(z * w, axis=0)
    sums = jnp.sum(all_ref[:, 0:wide].astype(f32).reshape(chips, rows, wide) * w, axis=0)
    inv = 1.0 / total
    f = sums[:, 0:feat] * inv
    at = iota((rows, heads * lat), 0)
    src = (at // per) * lat + group * per + at % per
    r = nn(one_hot(iota((rows, heads * lat), 1) == src), r_ref[...])
    delta = jnp.sum(f * r, axis=1, keepdims=True)
    g = sums[:, feat:wide] * inv - delta * f
    fb = f.astype(bf16)
    gb = g.astype(bf16)
    fg_out[...] = jnp.concatenate([fb, gb], axis=1)
    mine = iota((rows, width), 1) // HS == iota((rows, width), 0) // per
    o = jnp.where(mine, nn(fb, wv_ref[...]), 0.0).astype(bf16)
    dq = jnp.where(mine, nn(gb, wk_ref[...]) * (HS ** -0.5), 0.0).astype(bf16)
    up = nn(o, wo_ref[...])
    dn = nt(dq, wq_ref[...])
    up = up + pltpu.roll(up, per, 0)
    dn = dn + pltpu.roll(dn, per, 0)
    part_out[...] = jnp.where(iota(up.shape, 0) < per, up, dn).astype(bf16)


def spread_kernel(chips, heads, groups, core_ref, chip_ref, *refs):
    parts, (fg_ref, lat_ref, out_ref) = refs[:groups], refs[groups:]
    rows = fg_ref.shape[0]
    per = rows // heads
    lat = lat_ref.shape[0]
    group = core_ref[0] * chips + chip_ref[0]
    tot = parts[0][...].astype(f32)
    for p in parts[1:]:
        tot = tot + p[...].astype(f32)
    at = iota((rows, lat), 0)
    x = nn(one_hot(iota((rows, lat), 1) == group * per + at % per), lat_ref[...])
    mean = jnp.mean(x, axis=-1, keepdims=True)
    d = x - mean
    inv = lax.rsqrt(jnp.mean(d * d, axis=-1, keepdims=True) + 1e-5)
    xhat = d * inv
    back = inv * (tot - jnp.mean(tot, axis=-1, keepdims=True) - xhat * jnp.mean(tot * xhat, axis=-1, keepdims=True))
    ud = jnp.where(iota(tot.shape, 0) < per, tot, back)
    row = jnp.concatenate([fg_ref[...].astype(f32), ud], axis=1)
    block = jnp.concatenate([row, row], axis=0).astype(bf16)
    for s in range(chips // 2):
        out_ref[s * 2 * rows:(s + 1) * 2 * rows, :] = block


def finish_kernel(chips, heads, core_ref, own_ref, other_ref, q_ref, do_ref, latn_ref, wk_ref, wv_ref, du_ref,
                  up_out, dl_out, dwq_out, dwk_out, dwv_out, dwo_out):
    lat, width = q_ref.shape
    feat = wk_ref.shape[0]
    half = own_ref.shape[0]
    rows = half // chips
    per = rows // heads
    core = core_ref[0]

    def place(at):
        c = jnp.where(at < half, core, 1 - core)
        chip = (at % half) // rows
        return (c * chips + chip) * per + at % per, (at % rows) // per

    both = jnp.concatenate([own_ref[...], other_ref[...]], axis=0)
    f = both[:, 0:feat]
    g = both[:, feat:2 * feat]
    ud = both[:, 2 * feat:]
    l, _ = place(iota((2 * half, lat), 0))
    spread = one_hot(l == iota((2 * half, lat), 1))
    _, h = place(iota((2 * half, width), 0))
    mine = h == iota((2 * half, width), 1) // HS
    zero = jnp.zeros((), f32)
    do = jnp.where(mine, nn(spread, do_ref[...]), zero).astype(bf16)
    q = jnp.where(mine, nn(spread, q_ref[...]), zero).astype(bf16)
    dwv_out[...] = tn(f, do)
    dwk_out[...] = tn(g, q)
    o = jnp.where(mine, nn(f, wv_ref[...]), zero).astype(bf16)
    dq = jnp.where(mine, nn(g, wk_ref[...]) * (HS ** -0.5), zero).astype(bf16)
    l, h = place(iota((lat, 2 * half), 1))
    hit = l == iota((lat, 2 * half), 0)
    gather = one_hot(hit)
    o = nn(gather, o).astype(bf16)
    dq = nn(gather, dq).astype(bf16)
    dwo_out[...] = tn(o, du_ref[...])
    dwq_out[...] = tn(latn_ref[...], dq)
    up_out[...] = nn(one_hot(hit & (h == 0)), ud).astype(bf16)
    dl_out[...] = nn(one_hot(hit & (h == 1)), ud)


def small(kernel, outs, smem, name):
    one = pl.BlockSpec(memory_space=pltpu.VMEM)
    params = pltpu.CompilerParams(vmem_limit_bytes=VMEM)
    shapes = [jax.ShapeDtypeStruct(s, t) for s, t in outs]

    def call(*args):
        specs = [pl.BlockSpec(memory_space=pltpu.SMEM)] * smem + [one] * (len(args) - smem)
        return pl.pallas_call(
            kernel, out_shape=shapes, in_specs=specs, out_specs=[one] * len(shapes), compiler_params=params, name=name
        )(*args)

    return call


def shards(tokens, coords, latents, anchors, gamma, w_query, w_key, w_value, w_out, d_update):
    lat, dl = latents.shape
    feat = tokens.shape[1]
    heads = gamma.shape[0]
    width = heads * HS
    chips = lax.axis_size("chip")
    groups = lax.axis_size("head")
    half = heads * lat // 2
    rows = half // chips
    wide = 2 * feat
    core = lax.axis_index("core").astype(jnp.int32).reshape(1)
    chip = lax.axis_index("chip").astype(jnp.int32).reshape(1)
    swap = [(0, 1), (1, 0)]

    send, keep, latn, q, do, r = token_pass(
        core, gamma, tokens, coords, latents, anchors, w_query, w_key, w_value, w_out, d_update
    )
    got = lax.ppermute(send, "core", swap)
    (pair,) = small(pair_kernel, [((half, wide + STAT), bf16)], 0, "pair_sum")(keep, got)
    shares = lax.all_to_all(pair.reshape(chips, rows, wide + STAT), "chip", 0, 0, tiled=True)
    fg, part = small(
        functools.partial(owner_kernel, lat, heads, chips), [((rows, wide), bf16), ((rows, dl), bf16)], 2, "owner_rows"
    )(core, chip, shares.reshape(half, wide + STAT), r, w_key, w_value, w_out, w_query)
    parts = [part]
    for k in range(1, groups):
        parts.append(lax.ppermute(part, "head", [(i, (i + k) % groups) for i in range(groups)]))
    (copies,) = small(
        functools.partial(spread_kernel, chips, heads, groups), [((half, wide + dl), bf16)], 2, "spread_rows"
    )(core, chip, *parts, fg, latents)
    own = lax.all_to_all(copies.reshape(chips, rows, wide + dl), "chip", 0, 0, tiled=True).reshape(half, wide + dl)
    other = lax.ppermute(own, "core", swap)
    outs = [((lat, dl), bf16), ((lat, dl), f32), ((dl, width), f32), ((feat, width), f32), ((feat, width), f32), ((width, dl), f32)]
    return tuple(
        small(functools.partial(finish_kernel, chips, heads), outs, 1, "finish")(
            core, own, other, q, do, latn, w_key, w_value, d_update
        )
    )


def solution(mesh):
    toks, head = mesh.devices.shape
    fine = Mesh(mesh.devices.reshape(toks // 2, 2, head), ("chip", "core", "head"))
    tok = ("chip", "core")
    return jax.shard_map(
        shards,
        mesh=fine,
        in_specs=(
            P(tok, None),
            P(None, tok),
            P(),
            P(),
            P("head"),
            P(None, "head"),
            P(None, "head"),
            P(None, "head"),
            P("head", None),
            P(),
        ),
        out_specs=(P(), P(), P(None, "head"), P(None, "head"), P(None, "head"), P("head", None)),
        check_vma=False,
    )
```

```python
import functools

import jax
import jax.numpy as jnp
from jax import lax
from jax.experimental import pallas as pl
from jax.experimental.pallas import tpu as pltpu
from jax.sharding import Mesh, PartitionSpec as P

f32 = jnp.float32
bf16 = jnp.bfloat16
HS = 64
STAT = 128
Z_MIN = 1e-25
MAIN_VMEM = 58 * 1024 * 1024
VMEM = 10 * 1024 * 1024
NT = (((1,), (1,)), ((), ()))
TN = (((0,), (0,)), ((), ()))


def nn(a, b):
    return jnp.dot(a, b, preferred_element_type=f32)


def nt(a, b):
    return lax.dot_general(a, b, NT, preferred_element_type=f32)


def tn(a, b):
    return lax.dot_general(a, b, TN, preferred_element_type=f32)


def iota(shape, dim):
    return lax.broadcasted_iota(jnp.int32, shape, dim)


def one_hot(hit):
    return jnp.where(hit, 1.0, 0.0).astype(bf16)


def norm_rows(v):
    mean = jnp.mean(v, axis=-1, keepdims=True)
    d = v - mean
    var = jnp.mean(d * d, axis=-1, keepdims=True)
    return d * lax.rsqrt(var + 1e-5)


def column(row, n):
    return jnp.sum(
        jnp.where(iota((n, n), 0) == iota((n, n), 1), jnp.broadcast_to(row, (n, n)), 0.0), axis=1, keepdims=True
    )


def two_parts(v):
    high = v.astype(bf16).astype(f32)
    return high + (v - high).astype(bf16).astype(f32)


def token_kernel(lat, heads, tb, tc, core_ref, gamma_ref, tok_ref, pts_ref, lat_ref, anc_ref, wq_ref, wk_ref, wv_ref,
                 wo_ref, du_ref, send_ref, keep_ref, latn_out, q_out, do_out,
                 anc_s, p_s, r_s, shift_s, x_s, acc_s, z_s):
    step = pl.program_id(0)
    steps = pl.num_programs(0)
    rows = heads * lat
    feat = tok_ref.shape[1]

    @pl.when(step == 0)
    def _():
        latn = norm_rows(lat_ref[...].astype(f32)).astype(bf16)
        latn_out[...] = latn
        q = (nn(latn, wq_ref[...]) * (HS ** -0.5)).astype(bf16)
        do = nt(du_ref[...], wo_ref[...]).astype(bf16)
        q_out[...] = q
        do_out[...] = do
        box = jnp.zeros((lat, 1), f32)
        for k in range(3):
            a = column(anc_ref[k:k + 1, :], lat)
            anc_s[k] = jnp.broadcast_to(a, (lat, 128))
            low = jnp.min(pts_ref[k:k + 1, :], axis=1, keepdims=True)
            high = jnp.max(pts_ref[k:k + 1, :], axis=1, keepdims=True)
            gap = jnp.maximum(jnp.maximum(low - a, a - high), 0.0)
            box = box + gap * gap
        for h in range(heads):
            at = slice(h * lat, (h + 1) * lat)
            mine = iota(q.shape, 1) // HS == h
            p = nt(jnp.where(mine, q, jnp.zeros((), bf16)), wk_ref[...]).astype(bf16)
            r = nt(jnp.where(mine, do, jnp.zeros((), bf16)), wv_ref[...]).astype(bf16)
            p_s[at, :] = p
            r_s[at, :] = r
            size = p.astype(f32)
            size = jnp.sqrt(jnp.sum(size * size, axis=1, keepdims=True)) * (feat ** 0.5)
            shift_s[at, :] = jnp.broadcast_to(two_parts(size - gamma_ref[h] * box), (lat, 128))
        acc_s[...] = jnp.zeros_like(acc_s)
        z_s[...] = jnp.zeros_like(z_s)

    def wide(a):
        return jnp.concatenate([a] * (tc // 128), axis=1)

    def scores(x, pts):
        s = nt(p_s[...], x)
        dist = None
        for k in range(3):
            t = wide(anc_s[k]) - pts[k:k + 1, :]
            dist = t * t if dist is None else dist + t * t
        heads_s = []
        for h in range(heads):
            at = slice(h * lat, (h + 1) * lat)
            heads_s.append(s[at] - (gamma_ref[h] * dist + wide(shift_s[at, :])))
        return jnp.concatenate(heads_s, axis=0)

    def add_chunk(x, pts):
        s = scores(x, pts)
        g = nt(r_s[...], x)
        e = jnp.exp(s).astype(bf16)
        ef = e.astype(f32)
        part = ef[:, 0:128]
        for j in range(128, tc, 128):
            part = part + ef[:, j:j + 128]
        z_s[...] += part
        acc_s[...] += nn(jnp.concatenate([e, (ef * g).astype(bf16)], axis=0), x)

    start = pl.multiple_of(step * tb, tb)
    for t in range(0, tb, tc):
        x = norm_rows(tok_ref[t:t + tc, :].astype(f32)).astype(bf16)
        x_s[pl.ds(start + t, tc), :] = x
        add_chunk(x, pts_ref[:, pl.ds(start + t, tc)])

    @pl.when(step == steps - 1)
    def _():
        low = jnp.min(jnp.sum(z_s[...], axis=1, keepdims=True))

        @pl.when(jnp.logical_not(low >= Z_MIN))
        def _():
            chunks = x_s.shape[0] // tc
            shift_s[...] = jnp.zeros_like(shift_s)
            z_s[...] = jnp.full_like(z_s, -jnp.inf)

            def top(i, carry):
                at = pl.multiple_of(i * tc, tc)
                s = scores(x_s[pl.ds(at, tc), :], pts_ref[:, pl.ds(at, tc)])
                for j in range(0, tc, 128):
                    z_s[...] = jnp.maximum(z_s[...], s[:, j:j + 128])
                return carry

            lax.fori_loop(0, chunks, top, 0)
            shift_s[...] = jnp.broadcast_to(two_parts(jnp.max(z_s[...], axis=1, keepdims=True)), shift_s.shape)
            acc_s[...] = jnp.zeros_like(acc_s)
            z_s[...] = jnp.zeros_like(z_s)

            def again(i, carry):
                at = pl.multiple_of(i * tc, tc)
                add_chunk(x_s[pl.ds(at, tc), :], pts_ref[:, pl.ds(at, tc)])
                return carry

            lax.fori_loop(0, chunks, again, 0)

        stat = write_stat(jnp.sum(z_s[...], axis=1, keepdims=True), shift_s[:, 0:1])
        full = jnp.concatenate([acc_s[0:rows, :].astype(bf16), acc_s[rows:2 * rows, :].astype(bf16), stat], axis=1)
        core = core_ref[0]
        half = rows // 2
        per = 4
        at = iota((half, rows), 0)
        for out, c in ((send_ref, 1 - core), (keep_ref, core)):
            src = (at // per % heads) * lat + c * (lat // 2) + at // (per * heads) * per + at % per
            out[...] = nn(one_hot(iota((half, rows), 1) == src), full).astype(bf16)


def token_pass(core, gamma, tokens, coords, latents, anchors, wq, wk, wv, wo, du):
    toks, feat = tokens.shape
    lat, dl = latents.shape
    heads = gamma.shape[0]
    width = heads * HS
    rows = heads * lat
    tb = min(4096, toks)
    tc = min(256, tb)
    cols = 2 * feat + STAT

    def full(a):
        return pl.BlockSpec(a.shape, lambda i: (0,) * len(a.shape))

    smem = pl.BlockSpec(memory_space=pltpu.SMEM)
    shapes = [(rows // 2, cols)] * 2 + [(lat, dl), (lat, width), (lat, width)]
    outs = [jax.ShapeDtypeStruct(s, bf16) for s in shapes]
    held = (coords, latents, anchors, wq, wk, wv, wo, du)
    return pl.pallas_call(
        functools.partial(token_kernel, lat, heads, tb, tc),
        grid=(toks // tb,),
        out_shape=outs,
        in_specs=[smem, smem, pl.BlockSpec((tb, feat), lambda i: (i, 0))] + [full(a) for a in held],
        out_specs=[full(o) for o in outs],
        scratch_shapes=[
            pltpu.VMEM((3, lat, 128), f32),
            pltpu.VMEM((rows, feat), bf16),
            pltpu.VMEM((rows, feat), bf16),
            pltpu.VMEM((rows, 128), f32),
            pltpu.VMEM((toks, feat), bf16),
            pltpu.VMEM((2 * rows, feat), f32),
            pltpu.VMEM((rows, 128), f32),
        ],
        compiler_params=pltpu.CompilerParams(vmem_limit_bytes=MAIN_VMEM),
        name="token_pass",
    )(core, gamma, tokens, *held)


def read_stat(stat):
    return stat[:, 0:1] + stat[:, 1:2], stat[:, 2:3] + stat[:, 3:4]


def write_stat(z, shift):
    rows = z.shape[0]
    at = iota((rows, STAT), 1)
    z_hi = z.astype(bf16).astype(f32)
    s_hi = shift.astype(bf16).astype(f32)
    stat = jnp.where(at == 2, s_hi, jnp.where(at == 3, shift - s_hi, 0.0))
    stat = jnp.where(at == 0, z_hi, jnp.where(at == 1, z - z_hi, stat))
    return stat.astype(bf16)


def pair_kernel(a_ref, b_ref, out_ref):
    wide = a_ref.shape[1] - STAT
    za, sa = read_stat(a_ref[:, wide:].astype(f32))
    zb, sb = read_stat(b_ref[:, wide:].astype(f32))
    shift = jnp.maximum(sa, sb)
    wa = jnp.exp(sa - shift)
    wb = jnp.exp(sb - shift)
    out_ref[:, 0:wide] = (a_ref[:, 0:wide].astype(f32) * wa + b_ref[:, 0:wide].astype(f32) * wb).astype(bf16)
    out_ref[:, wide:] = write_stat(za * wa + zb * wb, shift)


def owner_kernel(lat, heads, chips, core_ref, chip_ref, all_ref, du_ref, wk_ref, wv_ref, wo_ref, wq_ref, fg_out, part_out):
    rows = all_ref.shape[0] // chips
    per = rows // heads
    feat = wk_ref.shape[0]
    width = wk_ref.shape[1]
    wide = 2 * feat
    group = core_ref[0] * chips + chip_ref[0]
    z, shift = read_stat(all_ref[:, wide:].astype(f32))
    z = z.reshape(chips, rows, 1)
    shift = shift.reshape(chips, rows, 1)
    top = jnp.max(shift, axis=0, keepdims=True)
    w = jnp.exp(shift - top)
    total = jnp.sum(z * w, axis=0)
    sums = jnp.sum(all_ref[:, 0:wide].astype(f32).reshape(chips, rows, wide) * w, axis=0)
    inv = 1.0 / total
    f = sums[:, 0:feat] * inv
    at = iota((rows, lat), 0)
    du = nn(one_hot(iota((rows, lat), 1) == group * per + at % per), du_ref[...]).astype(bf16)
    mine = iota((rows, width), 1) // HS == iota((rows, width), 0) // per
    do = jnp.where(mine, nt(du, wo_ref[...]), 0.0).astype(bf16)
    r = nt(do, wv_ref[...]).astype(bf16).astype(f32)
    delta = jnp.sum(f * r, axis=1, keepdims=True)
    g = sums[:, feat:wide] * inv - delta * f
    fb = f.astype(bf16)
    gb = g.astype(bf16)
    fg_out[...] = jnp.concatenate([fb, gb], axis=1)
    o = jnp.where(mine, nn(fb, wv_ref[...]), 0.0).astype(bf16)
    dq = jnp.where(mine, nn(gb, wk_ref[...]) * (HS ** -0.5), 0.0).astype(bf16)
    up = nn(o, wo_ref[...])
    dn = nt(dq, wq_ref[...])
    up = up + pltpu.roll(up, per, 0)
    dn = dn + pltpu.roll(dn, per, 0)
    part_out[...] = jnp.where(iota(up.shape, 0) < per, up, dn).astype(bf16)


def spread_kernel(chips, heads, groups, core_ref, chip_ref, *refs):
    parts, (fg_ref, lat_ref, out_ref) = refs[:groups], refs[groups:]
    rows = fg_ref.shape[0]
    per = rows // heads
    lat = lat_ref.shape[0]
    group = core_ref[0] * chips + chip_ref[0]
    tot = parts[0][...].astype(f32)
    for p in parts[1:]:
        tot = tot + p[...].astype(f32)
    at = iota((rows, lat), 0)
    x = nn(one_hot(iota((rows, lat), 1) == group * per + at % per), lat_ref[...])
    mean = jnp.mean(x, axis=-1, keepdims=True)
    d = x - mean
    inv = lax.rsqrt(jnp.mean(d * d, axis=-1, keepdims=True) + 1e-5)
    xhat = d * inv
    back = inv * (tot - jnp.mean(tot, axis=-1, keepdims=True) - xhat * jnp.mean(tot * xhat, axis=-1, keepdims=True))
    ud = jnp.where(iota(tot.shape, 0) < per, tot, back)
    row = jnp.concatenate([fg_ref[...].astype(f32), ud], axis=1)
    block = jnp.concatenate([row, row], axis=0).astype(bf16)
    for s in range(chips // 2):
        out_ref[s * 2 * rows:(s + 1) * 2 * rows, :] = block


def half_terms(chips, heads, core, rows_ref, q_ref, do_ref, wk_ref, wv_ref):
    lat, width = q_ref.shape
    feat = wk_ref.shape[0]
    half = rows_ref.shape[0]
    rows = half // chips
    per = rows // heads

    def latent(at):
        return (core * chips + at // rows) * per + at % per

    f = rows_ref[:, 0:feat]
    g = rows_ref[:, feat:2 * feat]
    ud = rows_ref[:, 2 * feat:]
    spread = one_hot(latent(iota((half, lat), 0)) == iota((half, lat), 1))
    mine = iota((half, width), 0) % rows // per == iota((half, width), 1) // HS
    zero = jnp.zeros((), f32)
    do = jnp.where(mine, nn(spread, do_ref[...]), zero).astype(bf16)
    q = jnp.where(mine, nn(spread, q_ref[...]), zero).astype(bf16)
    o = jnp.where(mine, nn(f, wv_ref[...]), zero).astype(bf16)
    dq = jnp.where(mine, nn(g, wk_ref[...]) * (HS ** -0.5), zero).astype(bf16)
    at = iota((lat, half), 1)
    hit = latent(at) == iota((lat, half), 0)
    gather = one_hot(hit)
    first = at % rows // per == 0
    return (
        tn(f, do),
        tn(g, q),
        nn(gather, o).astype(bf16),
        nn(gather, dq).astype(bf16),
        nn(one_hot(hit & first), ud).astype(bf16),
        nn(one_hot(hit & (at % rows // per == 1)), ud),
    )


def finish_own_kernel(chips, heads, core_ref, own_ref, q_ref, do_ref, wk_ref, wv_ref, *outs):
    for out, term in zip(outs, half_terms(chips, heads, core_ref[0], own_ref, q_ref, do_ref, wk_ref, wv_ref)):
        out[...] = term


def finish_kernel(chips, heads, core_ref, other_ref, q_ref, do_ref, wk_ref, wv_ref, latn_ref, du_ref,
                  dwv_ref, dwk_ref, o_ref, dq_ref, up_ref, dl_ref,
                  up_out, dl_out, dwq_out, dwk_out, dwv_out, dwo_out):
    dwv, dwk, o, dq, up, dl = half_terms(chips, heads, 1 - core_ref[0], other_ref, q_ref, do_ref, wk_ref, wv_ref)
    dwv_out[...] = dwv_ref[...] + dwv
    dwk_out[...] = dwk_ref[...] + dwk
    up_out[...] = up_ref[...] + up
    dl_out[...] = dl_ref[...] + dl
    dwo_out[...] = tn(o_ref[...] + o, du_ref[...])
    dwq_out[...] = tn(latn_ref[...], dq_ref[...] + dq)


def small(kernel, outs, smem, name):
    one = pl.BlockSpec(memory_space=pltpu.VMEM)
    params = pltpu.CompilerParams(vmem_limit_bytes=VMEM)
    shapes = [jax.ShapeDtypeStruct(s, t) for s, t in outs]

    def call(*args):
        specs = [pl.BlockSpec(memory_space=pltpu.SMEM)] * smem + [one] * (len(args) - smem)
        return pl.pallas_call(
            kernel, out_shape=shapes, in_specs=specs, out_specs=[one] * len(shapes), compiler_params=params, name=name,
            cost_estimate=pl.CostEstimate(flops=4 * 10 ** 8, bytes_accessed=10 ** 6, transcendentals=0),
        )(*args)

    return call


def shards(tokens, coords, latents, anchors, gamma, w_query, w_key, w_value, w_out, d_update):
    lat, dl = latents.shape
    feat = tokens.shape[1]
    heads = gamma.shape[0]
    width = heads * HS
    chips = lax.axis_size("chip")
    groups = lax.axis_size("head")
    half = heads * lat // 2
    rows = half // chips
    wide = 2 * feat
    core = lax.axis_index("core").astype(jnp.int32).reshape(1)
    chip = lax.axis_index("chip").astype(jnp.int32).reshape(1)
    swap = [(0, 1), (1, 0)]

    send, keep, latn, q, do = token_pass(
        core, gamma, tokens, coords, latents, anchors, w_query, w_key, w_value, w_out, d_update
    )
    got = lax.ppermute(send, "core", swap)
    (pair,) = small(pair_kernel, [((half, wide + STAT), bf16)], 0, "pair_sum")(keep.astype(f32), got)
    shares = lax.all_to_all(pair.reshape(chips, rows, wide + STAT), "chip", 0, 0, tiled=True)
    fg, part = small(
        functools.partial(owner_kernel, lat, heads, chips), [((rows, wide), bf16), ((rows, dl), bf16)], 2, "owner_rows"
    )(core, chip, shares.reshape(half, wide + STAT), d_update, w_key, w_value, w_out, w_query)
    parts = [part]
    for k in range(1, groups):
        parts.append(lax.ppermute(part, "head", [(i, (i + k) % groups) for i in range(groups)]))
    (copies,) = small(
        functools.partial(spread_kernel, chips, heads, groups), [((half, wide + dl), bf16)], 2, "spread_rows"
    )(core, chip, *parts, fg, latents)
    own = lax.all_to_all(copies.reshape(chips, rows, wide + dl), "chip", 0, 0, tiled=True).reshape(half, wide + dl)
    other = lax.ppermute(own, "core", swap)
    terms = [((feat, width), f32)] * 2 + [((lat, width), bf16)] * 2 + [((lat, dl), bf16), ((lat, dl), f32)]
    mine = small(functools.partial(finish_own_kernel, chips, heads), terms, 1, "finish_own")(
        core, own, q, do, w_key, w_value
    )
    outs = [((lat, dl), bf16), ((lat, dl), f32), ((dl, width), f32), ((feat, width), f32), ((feat, width), f32), ((width, dl), f32)]
    return tuple(
        small(functools.partial(finish_kernel, chips, heads), outs, 1, "finish")(
            core, other, q, do, w_key, w_value, latn, d_update, *mine
        )
    )


def solution(mesh):
    toks, head = mesh.devices.shape
    fine = Mesh(mesh.devices.reshape(toks // 2, 2, head), ("chip", "core", "head"))
    tok = ("chip", "core")
    return jax.shard_map(
        shards,
        mesh=fine,
        in_specs=(
            P(tok, None),
            P(None, tok),
            P(),
            P(),
            P("head"),
            P(None, "head"),
            P(None, "head"),
            P(None, "head"),
            P("head", None),
            P(),
        ),
        out_specs=(P(), P(), P(None, "head"), P(None, "head"), P(None, "head"), P("head", None)),
        check_vma=False,
    )
```

```python
import functools

import jax
import jax.numpy as jnp
from jax import lax
from jax.experimental import pallas as pl
from jax.experimental.pallas import tpu as pltpu
from jax.sharding import Mesh, PartitionSpec as P

f32 = jnp.float32
bf16 = jnp.bfloat16
HS = 64
STAT = 128
Z_MIN = 1e-25
MAIN_VMEM = 58 * 1024 * 1024
VMEM = 10 * 1024 * 1024
NT = (((1,), (1,)), ((), ()))
TN = (((0,), (0,)), ((), ()))


def nn(a, b):
    return jnp.dot(a, b, preferred_element_type=f32)


def nt(a, b):
    return lax.dot_general(a, b, NT, preferred_element_type=f32)


def tn(a, b):
    return lax.dot_general(a, b, TN, preferred_element_type=f32)


def iota(shape, dim):
    return lax.broadcasted_iota(jnp.int32, shape, dim)


def one_hot(hit):
    return jnp.where(hit, 1.0, 0.0).astype(bf16)


def norm_rows(v):
    mean = jnp.mean(v, axis=-1, keepdims=True)
    d = v - mean
    var = jnp.mean(d * d, axis=-1, keepdims=True)
    return d * lax.rsqrt(var + 1e-5)


def column(row, n):
    return jnp.sum(
        jnp.where(iota((n, n), 0) == iota((n, n), 1), jnp.broadcast_to(row, (n, n)), 0.0), axis=1, keepdims=True
    )


def two_parts(v):
    high = v.astype(bf16).astype(f32)
    return high + (v - high).astype(bf16).astype(f32)


def token_kernel(lat, heads, tb, tc, core_ref, gamma_ref, tok_ref, pts_ref, lat_ref, anc_ref, wq_ref, wk_ref, wv_ref,
                 wo_ref, du_ref, send_ref, keep_ref, latn_out, q_out, do_out,
                 anc_s, p_s, r_s, shift_s, x_s, acc_s, z_s):
    step = pl.program_id(0)
    steps = pl.num_programs(0)
    rows = heads * lat
    feat = tok_ref.shape[1]

    @pl.when(step == 0)
    def _():
        latn = norm_rows(lat_ref[...].astype(f32)).astype(bf16)
        latn_out[...] = latn
        q = (nn(latn, wq_ref[...]) * (HS ** -0.5)).astype(bf16)
        do = nt(du_ref[...], wo_ref[...]).astype(bf16)
        q_out[...] = q
        do_out[...] = do
        box = jnp.zeros((lat, 1), f32)
        for k in range(3):
            a = column(anc_ref[k:k + 1, :], lat)
            anc_s[k] = jnp.broadcast_to(a, (lat, 128))
            low = jnp.min(pts_ref[k:k + 1, :], axis=1, keepdims=True)
            high = jnp.max(pts_ref[k:k + 1, :], axis=1, keepdims=True)
            gap = jnp.maximum(jnp.maximum(low - a, a - high), 0.0)
            box = box + gap * gap
        for h in range(heads):
            at = slice(h * lat, (h + 1) * lat)
            mine = iota(q.shape, 1) // HS == h
            p = nt(jnp.where(mine, q, jnp.zeros((), bf16)), wk_ref[...]).astype(bf16)
            r = nt(jnp.where(mine, do, jnp.zeros((), bf16)), wv_ref[...]).astype(bf16)
            p_s[at, :] = p
            r_s[at, :] = r
            size = p.astype(f32)
            size = jnp.sqrt(jnp.sum(size * size, axis=1, keepdims=True)) * (feat ** 0.5 * (1 + 2 ** -8))
            shift_s[at, :] = jnp.broadcast_to(two_parts(size - gamma_ref[h] * box), (lat, 128))
        acc_s[...] = jnp.zeros_like(acc_s)
        z_s[...] = jnp.zeros_like(z_s)

    def wide(a):
        return jnp.concatenate([a] * (tc // 128), axis=1)

    def scores(x, pts):
        s = nt(p_s[...], x)
        dist = None
        for k in range(3):
            t = wide(anc_s[k]) - pts[k:k + 1, :]
            dist = t * t if dist is None else dist + t * t
        heads_s = []
        for h in range(heads):
            at = slice(h * lat, (h + 1) * lat)
            heads_s.append(s[at] - (gamma_ref[h] * dist + wide(shift_s[at, :])))
        return jnp.concatenate(heads_s, axis=0)

    def add_chunk(x, pts):
        s = scores(x, pts)
        g = nt(r_s[...], x)
        e = jnp.exp(s).astype(bf16)
        ef = e.astype(f32)
        part = ef[:, 0:128]
        for j in range(128, tc, 128):
            part = part + ef[:, j:j + 128]
        z_s[...] += part
        acc_s[...] += nn(jnp.concatenate([e, (ef * g).astype(bf16)], axis=0), x)

    start = pl.multiple_of(step * tb, tb)
    for t in range(0, tb, tc):
        x = norm_rows(tok_ref[t:t + tc, :].astype(f32)).astype(bf16)
        x_s[pl.ds(start + t, tc), :] = x
        add_chunk(x, pts_ref[:, pl.ds(start + t, tc)])

    @pl.when(step == steps - 1)
    def _():
        low = jnp.min(jnp.sum(z_s[...], axis=1, keepdims=True))

        @pl.when(jnp.logical_not(low >= Z_MIN))
        def _():
            chunks = x_s.shape[0] // tc
            shift_s[...] = jnp.zeros_like(shift_s)
            z_s[...] = jnp.full_like(z_s, -jnp.inf)

            def top(i, carry):
                at = pl.multiple_of(i * tc, tc)
                s = scores(x_s[pl.ds(at, tc), :], pts_ref[:, pl.ds(at, tc)])
                for j in range(0, tc, 128):
                    z_s[...] = jnp.maximum(z_s[...], s[:, j:j + 128])
                return carry

            lax.fori_loop(0, chunks, top, 0)
            shift_s[...] = jnp.broadcast_to(two_parts(jnp.max(z_s[...], axis=1, keepdims=True)), shift_s.shape)
            acc_s[...] = jnp.zeros_like(acc_s)
            z_s[...] = jnp.zeros_like(z_s)

            def again(i, carry):
                at = pl.multiple_of(i * tc, tc)
                add_chunk(x_s[pl.ds(at, tc), :], pts_ref[:, pl.ds(at, tc)])
                return carry

            lax.fori_loop(0, chunks, again, 0)

        stat = write_stat(jnp.sum(z_s[...], axis=1, keepdims=True), shift_s[:, 0:1])
        full = jnp.concatenate([acc_s[0:rows, :].astype(bf16), acc_s[rows:2 * rows, :].astype(bf16), stat], axis=1)
        core = core_ref[0]
        half = rows // 2
        per = 4
        at = iota((half, rows), 0)
        for out, c in ((send_ref, 1 - core), (keep_ref, core)):
            src = (at // per % heads) * lat + c * (lat // 2) + at // (per * heads) * per + at % per
            out[...] = nn(one_hot(iota((half, rows), 1) == src), full).astype(bf16)


def token_pass(core, gamma, tokens, coords, latents, anchors, wq, wk, wv, wo, du):
    toks, feat = tokens.shape
    lat, dl = latents.shape
    heads = gamma.shape[0]
    width = heads * HS
    rows = heads * lat
    tb = min(4096, toks)
    tc = min(256, tb)
    cols = 2 * feat + STAT

    def full(a):
        return pl.BlockSpec(a.shape, lambda i: (0,) * len(a.shape))

    smem = pl.BlockSpec(memory_space=pltpu.SMEM)
    shapes = [(rows // 2, cols)] * 2 + [(lat, dl), (lat, width), (lat, width)]
    outs = [jax.ShapeDtypeStruct(s, bf16) for s in shapes]
    held = (coords, latents, anchors, wq, wk, wv, wo, du)
    return pl.pallas_call(
        functools.partial(token_kernel, lat, heads, tb, tc),
        grid=(toks // tb,),
        out_shape=outs,
        in_specs=[smem, smem, pl.BlockSpec((tb, feat), lambda i: (i, 0))] + [full(a) for a in held],
        out_specs=[full(o) for o in outs],
        scratch_shapes=[
            pltpu.VMEM((3, lat, 128), f32),
            pltpu.VMEM((rows, feat), bf16),
            pltpu.VMEM((rows, feat), bf16),
            pltpu.VMEM((rows, 128), f32),
            pltpu.VMEM((toks, feat), bf16),
            pltpu.VMEM((2 * rows, feat), f32),
            pltpu.VMEM((rows, 128), f32),
        ],
        compiler_params=pltpu.CompilerParams(vmem_limit_bytes=MAIN_VMEM),
        name="token_pass",
    )(core, gamma, tokens, *held)


def read_stat(stat):
    return stat[:, 0:1] + stat[:, 1:2], stat[:, 2:3] + stat[:, 3:4]


def write_stat(z, shift):
    rows = z.shape[0]
    at = iota((rows, STAT), 1)
    z_hi = z.astype(bf16).astype(f32)
    s_hi = shift.astype(bf16).astype(f32)
    stat = jnp.where(at == 2, s_hi, jnp.where(at == 3, shift - s_hi, 0.0))
    stat = jnp.where(at == 0, z_hi, jnp.where(at == 1, z - z_hi, stat))
    return stat.astype(bf16)


def pair_kernel(a_ref, b_ref, out_ref):
    wide = a_ref.shape[1] - STAT
    za, sa = read_stat(a_ref[:, wide:].astype(f32))
    zb, sb = read_stat(b_ref[:, wide:].astype(f32))
    shift = jnp.maximum(sa, sb)
    wa = jnp.exp(sa - shift)
    wb = jnp.exp(sb - shift)
    out_ref[:, 0:wide] = (a_ref[:, 0:wide].astype(f32) * wa + b_ref[:, 0:wide].astype(f32) * wb).astype(bf16)
    out_ref[:, wide:] = write_stat(za * wa + zb * wb, shift)


def owner_kernel(lat, heads, chips, core_ref, chip_ref, all_ref, du_ref, wk_ref, wv_ref, wo_ref, wq_ref, fg_out, part_out):
    rows = all_ref.shape[0] // chips
    per = rows // heads
    feat = wk_ref.shape[0]
    width = wk_ref.shape[1]
    wide = 2 * feat
    group = core_ref[0] * chips + chip_ref[0]
    z, shift = read_stat(all_ref[:, wide:].astype(f32))
    z = z.reshape(chips, rows, 1)
    shift = shift.reshape(chips, rows, 1)
    top = jnp.max(shift, axis=0, keepdims=True)
    w = jnp.exp(shift - top)
    total = jnp.sum(z * w, axis=0)
    sums = jnp.sum(all_ref[:, 0:wide].astype(f32).reshape(chips, rows, wide) * w, axis=0)
    inv = 1.0 / total
    f = sums[:, 0:feat] * inv
    at = iota((rows, lat), 0)
    du = nn(one_hot(iota((rows, lat), 1) == group * per + at % per), du_ref[...]).astype(bf16)
    mine = iota((rows, width), 1) // HS == iota((rows, width), 0) // per
    do = jnp.where(mine, nt(du, wo_ref[...]), 0.0).astype(bf16)
    r = nt(do, wv_ref[...]).astype(bf16).astype(f32)
    delta = jnp.sum(f * r, axis=1, keepdims=True)
    g = sums[:, feat:wide] * inv - delta * f
    fb = f.astype(bf16)
    gb = g.astype(bf16)
    fg_out[...] = jnp.concatenate([fb, gb], axis=1)
    o = jnp.where(mine, nn(fb, wv_ref[...]), 0.0).astype(bf16)
    dq = jnp.where(mine, nn(gb, wk_ref[...]) * (HS ** -0.5), 0.0).astype(bf16)
    up = nn(o, wo_ref[...])
    dn = nt(dq, wq_ref[...])
    up = up + pltpu.roll(up, per, 0)
    dn = dn + pltpu.roll(dn, per, 0)
    part_out[...] = jnp.where(iota(up.shape, 0) < per, up, dn).astype(bf16)


def spread_kernel(chips, heads, groups, core_ref, chip_ref, *refs):
    parts, (fg_ref, lat_ref, out_ref) = refs[:groups], refs[groups:]
    rows = fg_ref.shape[0]
    per = rows // heads
    lat = lat_ref.shape[0]
    group = core_ref[0] * chips + chip_ref[0]
    tot = parts[0][...].astype(f32)
    for p in parts[1:]:
        tot = tot + p[...].astype(f32)
    at = iota((rows, lat), 0)
    x = nn(one_hot(iota((rows, lat), 1) == group * per + at % per), lat_ref[...])
    mean = jnp.mean(x, axis=-1, keepdims=True)
    d = x - mean
    inv = lax.rsqrt(jnp.mean(d * d, axis=-1, keepdims=True) + 1e-5)
    xhat = d * inv
    back = inv * (tot - jnp.mean(tot, axis=-1, keepdims=True) - xhat * jnp.mean(tot * xhat, axis=-1, keepdims=True))
    ud = jnp.where(iota(tot.shape, 0) < per, tot, back)
    row = jnp.concatenate([fg_ref[...].astype(f32), ud], axis=1)
    block = jnp.concatenate([row, row], axis=0).astype(bf16)
    for s in range(chips // 2):
        out_ref[s * 2 * rows:(s + 1) * 2 * rows, :] = block


def half_terms(chips, heads, core, rows_ref, q_ref, do_ref, wk_ref, wv_ref):
    lat, width = q_ref.shape
    feat = wk_ref.shape[0]
    half = rows_ref.shape[0]
    rows = half // chips
    per = rows // heads

    def latent(at):
        return (core * chips + at // rows) * per + at % per

    f = rows_ref[:, 0:feat]
    g = rows_ref[:, feat:2 * feat]
    ud = rows_ref[:, 2 * feat:]
    spread = one_hot(latent(iota((half, lat), 0)) == iota((half, lat), 1))
    mine = iota((half, width), 0) % rows // per == iota((half, width), 1) // HS
    zero = jnp.zeros((), f32)
    do = jnp.where(mine, nn(spread, do_ref[...]), zero).astype(bf16)
    q = jnp.where(mine, nn(spread, q_ref[...]), zero).astype(bf16)
    o = jnp.where(mine, nn(f, wv_ref[...]), zero).astype(bf16)
    dq = jnp.where(mine, nn(g, wk_ref[...]) * (HS ** -0.5), zero).astype(bf16)
    at = iota((lat, half), 1)
    hit = latent(at) == iota((lat, half), 0)
    gather = one_hot(hit)
    first = at % rows // per == 0
    return (
        tn(f, do),
        tn(g, q),
        nn(gather, o).astype(bf16),
        nn(gather, dq).astype(bf16),
        nn(one_hot(hit & first), ud).astype(bf16),
        nn(one_hot(hit & (at % rows // per == 1)), ud),
    )


def finish_own_kernel(chips, heads, core_ref, own_ref, q_ref, do_ref, wk_ref, wv_ref, *outs):
    for out, term in zip(outs, half_terms(chips, heads, core_ref[0], own_ref, q_ref, do_ref, wk_ref, wv_ref)):
        out[...] = term


def finish_kernel(chips, heads, core_ref, other_ref, q_ref, do_ref, wk_ref, wv_ref, latn_ref, du_ref,
                  dwv_ref, dwk_ref, o_ref, dq_ref, up_ref, dl_ref,
                  up_out, dl_out, dwq_out, dwk_out, dwv_out, dwo_out):
    dwv, dwk, o, dq, up, dl = half_terms(chips, heads, 1 - core_ref[0], other_ref, q_ref, do_ref, wk_ref, wv_ref)
    dwv_out[...] = dwv_ref[...] + dwv
    dwk_out[...] = dwk_ref[...] + dwk
    up_out[...] = up_ref[...] + up
    dl_out[...] = dl_ref[...] + dl
    dwo_out[...] = tn(o_ref[...] + o, du_ref[...])
    dwq_out[...] = tn(latn_ref[...], dq_ref[...] + dq)


def small(kernel, outs, smem, name):
    one = pl.BlockSpec(memory_space=pltpu.VMEM)
    params = pltpu.CompilerParams(vmem_limit_bytes=VMEM)
    shapes = [jax.ShapeDtypeStruct(s, t) for s, t in outs]

    def call(*args):
        specs = [pl.BlockSpec(memory_space=pltpu.SMEM)] * smem + [one] * (len(args) - smem)
        return pl.pallas_call(
            kernel, out_shape=shapes, in_specs=specs, out_specs=[one] * len(shapes), compiler_params=params, name=name,
            cost_estimate=pl.CostEstimate(flops=4 * 10 ** 8, bytes_accessed=10 ** 6, transcendentals=0),
        )(*args)

    return call


def shards(tokens, coords, latents, anchors, gamma, w_query, w_key, w_value, w_out, d_update):
    lat, dl = latents.shape
    feat = tokens.shape[1]
    heads = gamma.shape[0]
    width = heads * HS
    chips = lax.axis_size("chip")
    groups = lax.axis_size("head")
    half = heads * lat // 2
    rows = half // chips
    wide = 2 * feat
    core = lax.axis_index("core").astype(jnp.int32).reshape(1)
    chip = lax.axis_index("chip").astype(jnp.int32).reshape(1)
    swap = [(0, 1), (1, 0)]

    send, keep, latn, q, do = token_pass(
        core, gamma, tokens, coords, latents, anchors, w_query, w_key, w_value, w_out, d_update
    )
    got = lax.ppermute(send, "core", swap)
    (pair,) = small(pair_kernel, [((half, wide + STAT), bf16)], 0, "pair_sum")(keep.astype(f32), got)
    shares = lax.all_to_all(pair.reshape(chips, rows, wide + STAT), "chip", 0, 0, tiled=True)
    fg, part = small(
        functools.partial(owner_kernel, lat, heads, chips), [((rows, wide), bf16), ((rows, dl), bf16)], 2, "owner_rows"
    )(core, chip, shares.reshape(half, wide + STAT), d_update, w_key, w_value, w_out, w_query)
    parts = [part]
    for k in range(1, groups):
        parts.append(lax.ppermute(part, "head", [(i, (i + k) % groups) for i in range(groups)]))
    (copies,) = small(
        functools.partial(spread_kernel, chips, heads, groups), [((half, wide + dl), bf16)], 2, "spread_rows"
    )(core, chip, *parts, fg, latents)
    own = lax.all_to_all(copies.reshape(chips, rows, wide + dl), "chip", 0, 0, tiled=True).reshape(half, wide + dl)
    other = lax.ppermute(own, "core", swap)
    terms = [((feat, width), f32)] * 2 + [((lat, width), bf16)] * 2 + [((lat, dl), bf16), ((lat, dl), f32)]
    mine = small(functools.partial(finish_own_kernel, chips, heads), terms, 1, "finish_own")(
        core, own, q, do, w_key, w_value
    )
    outs = [((lat, dl), bf16), ((lat, dl), f32), ((dl, width), f32), ((feat, width), f32), ((feat, width), f32), ((width, dl), f32)]
    return tuple(
        small(functools.partial(finish_kernel, chips, heads), outs, 1, "finish")(
            core, other, q, do, w_key, w_value, latn, d_update, *mine
        )
    )


def solution(mesh):
    toks, head = mesh.devices.shape
    fine = Mesh(mesh.devices.reshape(toks // 2, 2, head), ("chip", "core", "head"))
    tok = ("chip", "core")
    return jax.shard_map(
        shards,
        mesh=fine,
        in_specs=(
            P(tok, None),
            P(None, tok),
            P(),
            P(),
            P("head"),
            P(None, "head"),
            P(None, "head"),
            P(None, "head"),
            P("head", None),
            P(),
        ),
        out_specs=(P(), P(), P(None, "head"), P(None, "head"), P(None, "head"), P("head", None)),
        check_vma=False,
    )
```

```python
import functools

import jax
import jax.numpy as jnp
from jax import lax
from jax.experimental import pallas as pl
from jax.experimental.pallas import tpu as pltpu
from jax.sharding import Mesh, PartitionSpec as P

f32 = jnp.float32
bf16 = jnp.bfloat16
HS = 64
STAT = 128
Z_MIN = 1e-25
MAIN_VMEM = 58 * 1024 * 1024
VMEM = 10 * 1024 * 1024
NT = (((1,), (1,)), ((), ()))
TN = (((0,), (0,)), ((), ()))


def nn(a, b):
    return jnp.dot(a, b, preferred_element_type=f32)


def nt(a, b):
    return lax.dot_general(a, b, NT, preferred_element_type=f32)


def tn(a, b):
    return lax.dot_general(a, b, TN, preferred_element_type=f32)


def iota(shape, dim):
    return lax.broadcasted_iota(jnp.int32, shape, dim)


def one_hot(hit):
    return jnp.where(hit, 1.0, 0.0).astype(bf16)


def norm_rows(v):
    mean = jnp.mean(v, axis=-1, keepdims=True)
    d = v - mean
    var = jnp.mean(d * d, axis=-1, keepdims=True)
    return d * lax.rsqrt(var + 1e-5)


def column(row, n):
    return jnp.sum(
        jnp.where(iota((n, n), 0) == iota((n, n), 1), jnp.broadcast_to(row, (n, n)), 0.0), axis=1, keepdims=True
    )


def two_parts(v):
    high = v.astype(bf16).astype(f32)
    return high + (v - high).astype(bf16).astype(f32)


def projections(lat_ref, du_ref, wq_ref, wo_ref):
    latn = norm_rows(lat_ref[...].astype(f32)).astype(bf16)
    q = (nn(latn, wq_ref[...]) * (HS ** -0.5)).astype(bf16)
    return latn, q, nt(du_ref[...], wo_ref[...]).astype(bf16)


def token_kernel(lat, heads, tb, tc, core_ref, gamma_ref, tok_ref, pts_ref, lat_ref, anc_ref, wq_ref, wk_ref, wv_ref,
                 wo_ref, du_ref, send_ref, keep_ref,
                 anc_s, p_s, r_s, shift_s, x_s, acc_s, z_s):
    step = pl.program_id(0)
    steps = pl.num_programs(0)
    rows = heads * lat
    feat = tok_ref.shape[1]

    @pl.when(step == 0)
    def _():
        _, q, do = projections(lat_ref, du_ref, wq_ref, wo_ref)
        box = jnp.zeros((lat, 1), f32)
        for k in range(3):
            a = column(anc_ref[k:k + 1, :], lat)
            anc_s[k] = jnp.broadcast_to(a, (lat, 128))
            low = jnp.min(pts_ref[k:k + 1, :], axis=1, keepdims=True)
            high = jnp.max(pts_ref[k:k + 1, :], axis=1, keepdims=True)
            gap = jnp.maximum(jnp.maximum(low - a, a - high), 0.0)
            box = box + gap * gap
        for h in range(heads):
            at = slice(h * lat, (h + 1) * lat)
            mine = iota(q.shape, 1) // HS == h
            p = nt(jnp.where(mine, q, jnp.zeros((), bf16)), wk_ref[...]).astype(bf16)
            r = nt(jnp.where(mine, do, jnp.zeros((), bf16)), wv_ref[...]).astype(bf16)
            p_s[at, :] = p
            r_s[at, :] = r
            size = p.astype(f32)
            size = jnp.sqrt(jnp.sum(size * size, axis=1, keepdims=True)) * (feat ** 0.5 * (1 + 2 ** -8))
            shift_s[at, :] = jnp.broadcast_to(two_parts(size - gamma_ref[h] * box), (lat, 128))
        acc_s[...] = jnp.zeros_like(acc_s)
        z_s[...] = jnp.zeros_like(z_s)

    def wide(a):
        return jnp.concatenate([a] * (tc // 128), axis=1)

    def scores(x, pts):
        s = nt(p_s[...], x)
        dist = None
        for k in range(3):
            t = wide(anc_s[k]) - pts[k:k + 1, :]
            dist = t * t if dist is None else dist + t * t
        heads_s = []
        for h in range(heads):
            at = slice(h * lat, (h + 1) * lat)
            heads_s.append(s[at] - (gamma_ref[h] * dist + wide(shift_s[at, :])))
        return jnp.concatenate(heads_s, axis=0)

    def add_chunk(x, pts):
        s = scores(x, pts)
        g = nt(r_s[...], x)
        e = jnp.exp(s).astype(bf16)
        ef = e.astype(f32)
        part = ef[:, 0:128]
        for j in range(128, tc, 128):
            part = part + ef[:, j:j + 128]
        z_s[...] += part
        acc_s[...] += nn(jnp.concatenate([e, (ef * g).astype(bf16)], axis=0), x)

    start = pl.multiple_of(step * tb, tb)
    for t in range(0, tb, tc):
        x = norm_rows(tok_ref[t:t + tc, :].astype(f32)).astype(bf16)
        x_s[pl.ds(start + t, tc), :] = x
        add_chunk(x, pts_ref[:, pl.ds(start + t, tc)])

    @pl.when(step == steps - 1)
    def _():
        low = jnp.min(jnp.sum(z_s[...], axis=1, keepdims=True))

        @pl.when(jnp.logical_not(low >= Z_MIN))
        def _():
            chunks = x_s.shape[0] // tc
            shift_s[...] = jnp.zeros_like(shift_s)
            z_s[...] = jnp.full_like(z_s, -jnp.inf)

            def top(i, carry):
                at = pl.multiple_of(i * tc, tc)
                s = scores(x_s[pl.ds(at, tc), :], pts_ref[:, pl.ds(at, tc)])
                for j in range(0, tc, 128):
                    z_s[...] = jnp.maximum(z_s[...], s[:, j:j + 128])
                return carry

            lax.fori_loop(0, chunks, top, 0)
            shift_s[...] = jnp.broadcast_to(two_parts(jnp.max(z_s[...], axis=1, keepdims=True)), shift_s.shape)
            acc_s[...] = jnp.zeros_like(acc_s)
            z_s[...] = jnp.zeros_like(z_s)

            def again(i, carry):
                at = pl.multiple_of(i * tc, tc)
                add_chunk(x_s[pl.ds(at, tc), :], pts_ref[:, pl.ds(at, tc)])
                return carry

            lax.fori_loop(0, chunks, again, 0)

        stat = write_stat(jnp.sum(z_s[...], axis=1, keepdims=True), shift_s[:, 0:1])
        full = jnp.concatenate([acc_s[0:rows, :].astype(bf16), acc_s[rows:2 * rows, :].astype(bf16), stat], axis=1)
        core = core_ref[0]
        half = rows // 2
        per = 4
        at = iota((half, rows), 0)
        for out, c in ((send_ref, 1 - core), (keep_ref, core)):
            src = (at // per % heads) * lat + c * (lat // 2) + at // (per * heads) * per + at % per
            out[...] = nn(one_hot(iota((half, rows), 1) == src), full).astype(bf16)


def token_pass(core, gamma, tokens, coords, latents, anchors, wq, wk, wv, wo, du):
    toks, feat = tokens.shape
    lat, dl = latents.shape
    heads = gamma.shape[0]
    width = heads * HS
    rows = heads * lat
    tb = min(4096, toks)
    tc = min(256, tb)
    cols = 2 * feat + STAT

    def full(a):
        return pl.BlockSpec(a.shape, lambda i: (0,) * len(a.shape))

    smem = pl.BlockSpec(memory_space=pltpu.SMEM)
    shapes = [(rows // 2, cols)] * 2
    outs = [jax.ShapeDtypeStruct(s, bf16) for s in shapes]
    held = (coords, latents, anchors, wq, wk, wv, wo, du)
    return pl.pallas_call(
        functools.partial(token_kernel, lat, heads, tb, tc),
        grid=(toks // tb,),
        out_shape=outs,
        in_specs=[smem, smem, pl.BlockSpec((tb, feat), lambda i: (i, 0))] + [full(a) for a in held],
        out_specs=[full(o) for o in outs],
        scratch_shapes=[
            pltpu.VMEM((3, lat, 128), f32),
            pltpu.VMEM((rows, feat), bf16),
            pltpu.VMEM((rows, feat), bf16),
            pltpu.VMEM((rows, 128), f32),
            pltpu.VMEM((toks, feat), bf16),
            pltpu.VMEM((2 * rows, feat), f32),
            pltpu.VMEM((rows, 128), f32),
        ],
        compiler_params=pltpu.CompilerParams(vmem_limit_bytes=MAIN_VMEM),
        name="token_pass",
    )(core, gamma, tokens, *held)


def read_stat(stat):
    return stat[:, 0:1] + stat[:, 1:2], stat[:, 2:3] + stat[:, 3:4]


def write_stat(z, shift):
    rows = z.shape[0]
    at = iota((rows, STAT), 1)
    z_hi = z.astype(bf16).astype(f32)
    s_hi = shift.astype(bf16).astype(f32)
    stat = jnp.where(at == 2, s_hi, jnp.where(at == 3, shift - s_hi, 0.0))
    stat = jnp.where(at == 0, z_hi, jnp.where(at == 1, z - z_hi, stat))
    return stat.astype(bf16)


def pair_kernel(a_ref, b_ref, out_ref):
    wide = a_ref.shape[1] - STAT
    za, sa = read_stat(a_ref[:, wide:].astype(f32))
    zb, sb = read_stat(b_ref[:, wide:].astype(f32))
    shift = jnp.maximum(sa, sb)
    wa = jnp.exp(sa - shift)
    wb = jnp.exp(sb - shift)
    out_ref[:, 0:wide] = (a_ref[:, 0:wide].astype(f32) * wa + b_ref[:, 0:wide].astype(f32) * wb).astype(bf16)
    out_ref[:, wide:] = write_stat(za * wa + zb * wb, shift)


def owner_kernel(lat, heads, chips, core_ref, chip_ref, all_ref, du_ref, wk_ref, wv_ref, wo_ref, wq_ref, fg_out, part_out):
    rows = all_ref.shape[0] // chips
    per = rows // heads
    feat = wk_ref.shape[0]
    width = wk_ref.shape[1]
    wide = 2 * feat
    group = core_ref[0] * chips + chip_ref[0]
    z, shift = read_stat(all_ref[:, wide:].astype(f32))
    z = z.reshape(chips, rows, 1)
    shift = shift.reshape(chips, rows, 1)
    top = jnp.max(shift, axis=0, keepdims=True)
    w = jnp.exp(shift - top)
    total = jnp.sum(z * w, axis=0)
    sums = jnp.sum(all_ref[:, 0:wide].astype(f32).reshape(chips, rows, wide) * w, axis=0)
    inv = 1.0 / total
    f = sums[:, 0:feat] * inv
    at = iota((rows, lat), 0)
    du = nn(one_hot(iota((rows, lat), 1) == group * per + at % per), du_ref[...]).astype(bf16)
    mine = iota((rows, width), 1) // HS == iota((rows, width), 0) // per
    do = jnp.where(mine, nt(du, wo_ref[...]), 0.0).astype(bf16)
    r = nt(do, wv_ref[...]).astype(bf16).astype(f32)
    delta = jnp.sum(f * r, axis=1, keepdims=True)
    g = sums[:, feat:wide] * inv - delta * f
    fb = f.astype(bf16)
    gb = g.astype(bf16)
    fg_out[...] = jnp.concatenate([fb, gb], axis=1)
    o = jnp.where(mine, nn(fb, wv_ref[...]), 0.0).astype(bf16)
    dq = jnp.where(mine, nn(gb, wk_ref[...]) * (HS ** -0.5), 0.0).astype(bf16)
    up = nn(o, wo_ref[...])
    dn = nt(dq, wq_ref[...])
    up = up + pltpu.roll(up, per, 0)
    dn = dn + pltpu.roll(dn, per, 0)
    part_out[...] = jnp.where(iota(up.shape, 0) < per, up, dn).astype(bf16)


def spread_kernel(chips, heads, groups, core_ref, chip_ref, *refs):
    parts, (fg_ref, lat_ref, out_ref) = refs[:groups], refs[groups:]
    rows = fg_ref.shape[0]
    per = rows // heads
    lat = lat_ref.shape[0]
    group = core_ref[0] * chips + chip_ref[0]
    tot = parts[0][...].astype(f32)
    for p in parts[1:]:
        tot = tot + p[...].astype(f32)
    at = iota((rows, lat), 0)
    x = nn(one_hot(iota((rows, lat), 1) == group * per + at % per), lat_ref[...])
    mean = jnp.mean(x, axis=-1, keepdims=True)
    d = x - mean
    inv = lax.rsqrt(jnp.mean(d * d, axis=-1, keepdims=True) + 1e-5)
    xhat = d * inv
    back = inv * (tot - jnp.mean(tot, axis=-1, keepdims=True) - xhat * jnp.mean(tot * xhat, axis=-1, keepdims=True))
    ud = jnp.where(iota(tot.shape, 0) < per, tot, back)
    row = jnp.concatenate([fg_ref[...].astype(f32), ud], axis=1)
    block = jnp.concatenate([row, row], axis=0).astype(bf16)
    for s in range(chips // 2):
        out_ref[s * 2 * rows:(s + 1) * 2 * rows, :] = block


def half_terms(chips, heads, core, rows_ref, q_all, do_all, wk_ref, wv_ref):
    lat, width = q_all.shape
    feat = wk_ref.shape[0]
    half = rows_ref.shape[0]
    rows = half // chips
    per = rows // heads

    def latent(at):
        return (core * chips + at // rows) * per + at % per

    f = rows_ref[:, 0:feat]
    g = rows_ref[:, feat:2 * feat]
    ud = rows_ref[:, 2 * feat:]
    spread = one_hot(latent(iota((half, lat), 0)) == iota((half, lat), 1))
    mine = iota((half, width), 0) % rows // per == iota((half, width), 1) // HS
    zero = jnp.zeros((), f32)
    do = jnp.where(mine, nn(spread, do_all), zero).astype(bf16)
    q = jnp.where(mine, nn(spread, q_all), zero).astype(bf16)
    o = jnp.where(mine, nn(f, wv_ref[...]), zero).astype(bf16)
    dq = jnp.where(mine, nn(g, wk_ref[...]) * (HS ** -0.5), zero).astype(bf16)
    at = iota((lat, half), 1)
    hit = latent(at) == iota((lat, half), 0)
    gather = one_hot(hit)
    first = at % rows // per == 0
    return (
        tn(f, do),
        tn(g, q),
        nn(gather, o).astype(bf16),
        nn(gather, dq).astype(bf16),
        nn(one_hot(hit & first), ud).astype(bf16),
        nn(one_hot(hit & (at % rows // per == 1)), ud),
    )


def finish_own_kernel(chips, heads, core_ref, own_ref, lat_ref, du_ref, wq_ref, wo_ref, wk_ref, wv_ref, *outs):
    latn, q, do = projections(lat_ref, du_ref, wq_ref, wo_ref)
    terms = (latn, q, do) + half_terms(chips, heads, core_ref[0], own_ref, q, do, wk_ref, wv_ref)
    for out, term in zip(outs, terms):
        out[...] = term


def finish_kernel(chips, heads, core_ref, other_ref, wk_ref, wv_ref, du_ref, latn_ref, q_ref, do_ref,
                  dwv_ref, dwk_ref, o_ref, dq_ref, up_ref, dl_ref,
                  up_out, dl_out, dwq_out, dwk_out, dwv_out, dwo_out):
    dwv, dwk, o, dq, up, dl = half_terms(chips, heads, 1 - core_ref[0], other_ref, q_ref[...], do_ref[...], wk_ref, wv_ref)
    dwv_out[...] = dwv_ref[...] + dwv
    dwk_out[...] = dwk_ref[...] + dwk
    up_out[...] = up_ref[...] + up
    dl_out[...] = dl_ref[...] + dl
    dwo_out[...] = tn(o_ref[...] + o, du_ref[...])
    dwq_out[...] = tn(latn_ref[...], dq_ref[...] + dq)


def small(kernel, outs, smem, name):
    one = pl.BlockSpec(memory_space=pltpu.VMEM)
    params = pltpu.CompilerParams(vmem_limit_bytes=VMEM)
    shapes = [jax.ShapeDtypeStruct(s, t) for s, t in outs]

    def call(*args):
        specs = [pl.BlockSpec(memory_space=pltpu.SMEM)] * smem + [one] * (len(args) - smem)
        return pl.pallas_call(
            kernel, out_shape=shapes, in_specs=specs, out_specs=[one] * len(shapes), compiler_params=params, name=name,
            cost_estimate=pl.CostEstimate(flops=4 * 10 ** 8, bytes_accessed=10 ** 6, transcendentals=0),
        )(*args)

    return call


def shards(tokens, coords, latents, anchors, gamma, w_query, w_key, w_value, w_out, d_update):
    lat, dl = latents.shape
    feat = tokens.shape[1]
    heads = gamma.shape[0]
    width = heads * HS
    chips = lax.axis_size("chip")
    groups = lax.axis_size("head")
    half = heads * lat // 2
    rows = half // chips
    wide = 2 * feat
    core = lax.axis_index("core").astype(jnp.int32).reshape(1)
    chip = lax.axis_index("chip").astype(jnp.int32).reshape(1)
    swap = [(0, 1), (1, 0)]

    send, keep = token_pass(
        core, gamma, tokens, coords, latents, anchors, w_query, w_key, w_value, w_out, d_update
    )
    got = lax.ppermute(send, "core", swap)
    (pair,) = small(pair_kernel, [((half, wide + STAT), bf16)], 0, "pair_sum")(keep.astype(f32), got)
    shares = lax.all_to_all(pair.reshape(chips, rows, wide + STAT), "chip", 0, 0, tiled=True)
    fg, part = small(
        functools.partial(owner_kernel, lat, heads, chips), [((rows, wide), bf16), ((rows, dl), bf16)], 2, "owner_rows"
    )(core, chip, shares.reshape(half, wide + STAT), d_update, w_key, w_value, w_out, w_query)
    parts = [part]
    for k in range(1, groups):
        parts.append(lax.ppermute(part, "head", [(i, (i + k) % groups) for i in range(groups)]))
    (copies,) = small(
        functools.partial(spread_kernel, chips, heads, groups), [((half, wide + dl), bf16)], 2, "spread_rows"
    )(core, chip, *parts, fg, latents)
    own = lax.all_to_all(copies.reshape(chips, rows, wide + dl), "chip", 0, 0, tiled=True).reshape(half, wide + dl)
    other = lax.ppermute(own, "core", swap)
    terms = [((lat, dl), bf16), ((lat, width), bf16), ((lat, width), bf16)] + [((feat, width), f32)] * 2 + [((lat, width), bf16)] * 2 + [((lat, dl), bf16), ((lat, dl), f32)]
    mine = small(functools.partial(finish_own_kernel, chips, heads), terms, 1, "finish_own")(
        core, own, latents, d_update, w_query, w_out, w_key, w_value
    )
    outs = [((lat, dl), bf16), ((lat, dl), f32), ((dl, width), f32), ((feat, width), f32), ((feat, width), f32), ((width, dl), f32)]
    return tuple(
        small(functools.partial(finish_kernel, chips, heads), outs, 1, "finish")(
            core, other, w_key, w_value, d_update, *mine
        )
    )


def solution(mesh):
    toks, head = mesh.devices.shape
    fine = Mesh(mesh.devices.reshape(toks // 2, 2, head), ("chip", "core", "head"))
    tok = ("chip", "core")
    return jax.shard_map(
        shards,
        mesh=fine,
        in_specs=(
            P(tok, None),
            P(None, tok),
            P(),
            P(),
            P("head"),
            P(None, "head"),
            P(None, "head"),
            P(None, "head"),
            P("head", None),
            P(),
        ),
        out_specs=(P(), P(), P(None, "head"), P(None, "head"), P(None, "head"), P("head", None)),
        check_vma=False,
    )
```
